128 devices in a mesh: ctx: 16 (over z, y), grp: 8 (over x, core).
Axes of the slice: x: 4, y: 4, z: 4, core: 2. Of those that a mesh axis runs over, the one named last changes fastest.
Arguments:
- tokens: bfloat16 [8192, 7168], P('ctx', 'grp'), may hold values from -6 to 6
- w_dkv: bfloat16 [7168, 576], P('grp'), may hold values from -0.0625 to 0.0625
- latent_gain: float32 [512], replicated, may hold values from 0.25 to 1.75
- q_pre: bfloat16 [8192, 73728], P('ctx', 'grp'), may hold values from -102 to 102
- w_uv: bfloat16 [512, 16384], P(None, 'grp'), may hold values from -0.25 to 0.25
- q_dec: bfloat16 [2, 128, 73728], P(None, 'grp'), may hold values from -102 to 102
- kv_new: bfloat16 [2, 128, 576], P(None, 'grp'), may hold values from -48 to 48
- lengths: int32 [128], P('grp'), may hold values from 1 to 8192
- block_map: int32 [256], replicated, may hold values from 0 to 15, as said below
Outputs:
- prefill_out: bfloat16 [8192, 16384], P('ctx', 'grp')
- decode_cache: bfloat16 [8192, 576], P('ctx')
- decode_out: bfloat16 [2, 128, 65536], P(None, 'grp', 'ctx')
The draws below stay inside these ranges and needn't reach their ends.
Inputs may be any that keep to these rules, and one draw needn't show every extreme that they name: `block_map`: for each index o of ctx, the 16 entries o*16 to o*16 + 15 name every shard number 0 to 15 exactly once.
All inputs are finite; a program needn't handle non-finite values.
Results may differ from the reference program's by a relative error of at most 0.012.
The reference program's roundings to bfloat16 on the way count: a program that leaves them out, or rounds other values in their place, can miss the bound.
Values may be sent and summed in bfloat16 or wider, within the bound.
A program may use at most 128 MiB of HBM per device.

```python
import jax
import jax.numpy as jnp
from jax import lax

D = 7168
H = 128
KV_RANK = 512
VHEAD = 128
BLOCK = 128
STEPS = 2
LATENT = 576
LEN = 8192
NBLK = 64
PAGE = 32
NPAGE = 256
REQS = 128
N_CTX = 16


def query_values(key, shape):
    base = jnp.clip(jax.random.normal(jax.random.fold_in(key, 3), shape, jnp.float32), -6.0, 6.0)
    return base.astype(jnp.bfloat16)


def draw_q_pre(key, part):
    key = jax.random.fold_in(key, 11)
    return query_values(key, (LEN, H * LATENT))


def draw_q_dec(key, part):
    key = jax.random.fold_in(key, 12)
    return query_values(key, (STEPS, REQS, H * LATENT))


def draw_lengths(key, part):
    key = jax.random.fold_in(key, 13)
    values = jax.random.randint(key, (REQS,), 1, LEN + 1, dtype=jnp.int32)
    spot = jax.random.randint(jax.random.fold_in(key, 1), (), 0, REQS, dtype=jnp.int32)
    return values.at[spot].set(LEN).astype(jnp.int32)


def draw_block_map(key, part):
    key = jax.random.fold_in(key, 14)
    shards = NPAGE // N_CTX
    owner_keys = jax.random.split(jax.random.fold_in(key, 1), shards)

    def one_owner(owner_key):
        return jax.random.permutation(owner_key, shards).astype(jnp.int32)
    table = jax.vmap(one_owner)(owner_keys)
    return table.reshape(NPAGE).astype(jnp.int32)


def block_levels(rng, extent, cuts, least, top_value):
    def one(position, shards_of):
        draws = jax.random.uniform(jax.random.fold_in(jax.random.fold_in(rng, 6), position), (shards_of,), jnp.float32, least / len(cuts), top_value / len(cuts))
        return jnp.repeat(jnp.exp(draws), extent[position] // shards_of).reshape((-1,) + (1,) * (len(extent) - position - 1))

    level = one(*cuts[0])
    for cut in cuts[1:]:
        level = level * one(*cut)
    return level


def centred(stream_key, extent, spread, most, cuts=(), held_as=jnp.bfloat16):
    values = spread * jax.random.normal(stream_key, extent, jnp.float32)
    if cuts:
        values = values * block_levels(stream_key, extent, cuts, -0.22, 0.18)
    return jnp.clip(values, -most, most).astype(held_as)


def setup_inputs(seed: int = 0) -> dict:
    splits = jax.random.split(jax.random.key(seed), 10)
    return {
        "tokens": centred(splits[0], (LEN, D), 1.0, 6.0, ((0, 16), (1, 8))),
        "w_dkv": centred(splits[1], (D, LATENT), D ** -0.5, 0.0625, ((0, 8),)),
        "latent_gain": jnp.clip(1.0 + 0.15 * jax.random.normal(splits[2], (KV_RANK,), jnp.float32), 0.25, 1.75),
        "q_pre": draw_q_pre(jax.random.fold_in(splits[9], 71), 0),
        "w_uv": centred(splits[4], (KV_RANK, H * VHEAD), KV_RANK ** -0.5, 0.25, ((1, 8),)),
        "q_dec": draw_q_dec(jax.random.fold_in(splits[9], 71), 0),
        "kv_new": centred(splits[6], (STEPS, REQS, LATENT), 8.0, 48.0, ((1, 8),)),
        "lengths": draw_lengths(jax.random.fold_in(splits[9], 71), 0),
        "block_map": draw_block_map(jax.random.fold_in(splits[9], 71), 0),
    }


scale_qk = 0.07216878364870322
eps_norm = 1e-06
neg_fill = -1e+30

def rotate(values, positions):
    half = values.shape[1] // 2
    freqs = 10000.0 ** (-(jnp.arange(half, dtype=jnp.float32) * 2.0) / (2.0 * half))
    angles = positions.astype(jnp.float32)[:, None] * freqs[None, :]
    cosine = jnp.cos(angles)
    sine = jnp.sin(angles)
    first = values[:, :half]
    second = values[:, half:]
    return jnp.concatenate([first * cosine - second * sine, second * cosine + first * sine], axis=1)

def make_rows(summed, gain, positions, rank):
    latent = summed[:, :rank]
    power = lax.optimization_barrier(jnp.mean(latent * latent, axis=1, keepdims=True))
    normed = latent * lax.rsqrt(power + eps_norm) * gain[None, :]
    return jnp.concatenate([normed, rotate(summed[:, rank:], positions)], axis=1).astype(jnp.bfloat16)

def reference(tokens, w_dkv, latent_gain, q_pre, w_uv, q_dec, kv_new, lengths, block_map):
    summed = jnp.dot(tokens, w_dkv, preferred_element_type=jnp.float32)
    rows = make_rows(summed, latent_gain, jnp.arange(LEN, dtype=jnp.int32), KV_RANK)
    padded = jnp.concatenate([jnp.zeros((BLOCK, LATENT), jnp.bfloat16), rows], axis=0)
    values_up = w_uv.astype(jnp.float32).reshape(KV_RANK, H, VHEAD)
    qrow = jnp.arange(BLOCK, dtype=jnp.int32)[:, None]
    kcol = jnp.arange(2 * BLOCK, dtype=jnp.int32)[None, :]

    def one_block(index):
        keys = lax.dynamic_slice_in_dim(padded, (index * BLOCK).astype(jnp.int32), 2 * BLOCK, 0)
        queries = lax.dynamic_slice_in_dim(q_pre, (index * BLOCK).astype(jnp.int32), BLOCK, 0)
        queries = queries.astype(jnp.float32).reshape(BLOCK, H, LATENT)
        scores = scale_qk * jnp.einsum('qhd,jd->hqj', queries, keys.astype(jnp.float32), precision=lax.Precision.HIGHEST)
        allowed = jnp.where(kcol < BLOCK, index > 0, kcol - BLOCK <= qrow)
        masked = jnp.where(allowed[None], scores, neg_fill)
        peak = lax.optimization_barrier(jnp.max(masked, axis=2, keepdims=True))
        expo = jnp.where(allowed[None], jnp.exp(masked - peak), 0.0)
        weights = (expo / lax.optimization_barrier(jnp.sum(expo, axis=2, keepdims=True))).astype(jnp.bfloat16)
        latent_out = jnp.einsum('hqj,jr->qhr', weights.astype(jnp.float32), keys[:, :KV_RANK].astype(jnp.float32), precision=lax.Precision.HIGHEST).astype(jnp.bfloat16)
        result = jnp.einsum('qhr,rhv->qhv', latent_out.astype(jnp.float32), values_up, precision=lax.Precision.HIGHEST)
        return result.astype(jnp.bfloat16).reshape(BLOCK, H * VHEAD)
    prefill_out = lax.map(one_block, jnp.arange(NBLK, dtype=jnp.int32)).reshape(LEN, H * VHEAD)
    order = jnp.argsort(block_map, stable=True)
    decode_cache = rows.reshape(NPAGE, PAGE, LATENT)[order].reshape(LEN, LATENT)
    rows_wide = rows.astype(jnp.float32)
    key_pos = jnp.arange(LEN, dtype=jnp.int32)
    own_mask = jnp.arange(STEPS)[None, :] <= jnp.arange(STEPS)[:, None]

    def one_request(index):
        queries = q_dec[:, index].astype(jnp.float32).reshape(STEPS, H, LATENT)
        fresh = kv_new[:, index].astype(jnp.float32)
        live = key_pos < lengths[index]
        s_pre = scale_qk * jnp.einsum('shd,jd->shj', queries, rows_wide, precision=lax.Precision.HIGHEST)
        s_new = scale_qk * jnp.einsum('shd,td->sht', queries, fresh, precision=lax.Precision.HIGHEST)
        m_pre = jnp.where(live[None, None, :], s_pre, neg_fill)
        m_new = jnp.where(own_mask[:, None, :], s_new, neg_fill)
        peak = jnp.maximum(lax.optimization_barrier(jnp.max(m_pre, axis=2)), lax.optimization_barrier(jnp.max(m_new, axis=2)))
        e_pre = jnp.where(live[None, None, :], jnp.exp(m_pre - peak[..., None]), 0.0)
        e_new = jnp.where(own_mask[:, None, :], jnp.exp(m_new - peak[..., None]), 0.0)
        total = lax.optimization_barrier(jnp.sum(e_pre, axis=2)) + lax.optimization_barrier(jnp.sum(e_new, axis=2))
        w_pre = lax.optimization_barrier(e_pre.astype(jnp.bfloat16)).astype(jnp.float32)
        w_new = lax.optimization_barrier(e_new.astype(jnp.bfloat16)).astype(jnp.float32)
        acc = jnp.einsum('shj,jc->shc', w_pre, rows_wide[:, :KV_RANK], precision=lax.Precision.HIGHEST)
        acc = acc + jnp.einsum('sht,tc->shc', w_new, fresh[:, :KV_RANK], precision=lax.Precision.HIGHEST)
        return (acc / total[..., None]).astype(jnp.bfloat16).reshape(STEPS, H * KV_RANK)
    decode_out = jnp.transpose(lax.map(one_request, jnp.arange(REQS, dtype=jnp.int32)), (1, 0, 2))
    return (prefill_out, decode_cache, decode_out)
```

```python
import math

import jax
import jax.numpy as jnp
import numpy as np
from jax import lax
from jax.experimental import pallas as pl
from jax.experimental.pallas import tpu as pltpu
from jax.sharding import PartitionSpec as P

MESH = pl.DeviceIdType.MESH
F32 = jnp.float32
BF16 = jnp.bfloat16

scale_qk = 0.07216878364870322
eps_norm = 1e-06
neg_fill = -1e30
EXP2_SCALE = scale_qk * math.log2(math.e)

RANK = 512
WIDTH = 576
WIDE = 640
ROPE = 64
BLOCK = 128
PIECE = 16
GROUPS = 4
GROUP_ROWS = 1024
HEADS = 16
DEC_HEADS = 8

ORDERS = (
    ("yzx", "zyx"),
    ("zxy", "xzy"),
    ("yxz", "xyz"),
    ("xzy", "xyz"),
)
POS_STRIDE = {"z": 2048, "y": 512, "x": 32}
SLOT_STRIDE = (PIECE, 4 * PIECE, 16 * PIECE)
DELTAS = (1, 3, 2)
FREQS = [float(np.float32(10000.0 ** (-2.0 * i / ROPE))) for i in range(ROPE // 2)]


def dot_nt(a, b):
    return lax.dot_general(a, b, (((1,), (1,)), ((), ())), preferred_element_type=F32)


def dot_nn(a, b):
    return jnp.dot(a, b, preferred_element_type=F32)


def kernel(
    tokens,
    w_dkv,
    gain,
    q_pre,
    w_uv,
    q_dec,
    kv_new,
    lengths,
    block_map,
    o_pre,
    o_cache,
    o_dec,
    tok_v,
    w_v,
    q_v,
    uv_v,
    qd_v,
    kv_v,
    part,
    from_core,
    chip_sum,
    from_x,
    buf,
    win,
    qs,
    kn,
    acc,
    top,
    total,
    out_v,
    cache_v,
    dec_v,
    load_sem,
    core_send,
    core_recv,
    x_send,
    x_recv,
    g_send,
    g_recv,
    f_send,
    f_recv,
    out_sem,
):
    ctx = lax.axis_index("ctx")
    grp = lax.axis_index("grp")
    at = {"z": ctx // 4, "y": lax.rem(ctx, 4), "x": grp // 2}
    core = lax.rem(grp, 2)
    other = 1 - core

    def device(x, y, z, c):
        return (z * 4 + y, x * 2 + c)

    def moved(axis, delta):
        new = dict(at)
        new[axis] = lax.rem(at[axis] + delta, 4)
        return device(new["x"], new["y"], new["z"], core)

    sibling = device(at["x"], at["y"], at["z"], other)

    loads = {
        "tok": pltpu.make_async_copy(tokens, tok_v, load_sem.at[0]),
        "w": pltpu.make_async_copy(w_dkv, w_v, load_sem.at[1]),
        "qd": pltpu.make_async_copy(
            q_dec.at[:, :, pl.ds(pl.multiple_of(ctx * (DEC_HEADS * WIDTH), 128), DEC_HEADS * WIDTH)],
            qd_v,
            load_sem.at[2],
        ),
        "kv": pltpu.make_async_copy(kv_new, kv_v, load_sem.at[3]),
        "q": pltpu.make_async_copy(q_pre, q_v, load_sem.at[4]),
        "uv": pltpu.make_async_copy(w_uv, uv_v, load_sem.at[5]),
    }
    for load in loads.values():
        load.start()

    barrier = pltpu.get_barrier_semaphore()
    peers = [sibling] + [moved(axis, delta) for axis in "xyz" for delta in DELTAS]
    for peer in peers:
        pl.semaphore_signal(barrier, inc=1, device_id=peer, device_id_type=MESH)

    def remote(src, dst, send, recv, to):
        return pltpu.make_async_remote_copy(
            src_ref=src, dst_ref=dst, send_sem=send, recv_sem=recv, device_id=to, device_id_type=MESH
        )

    lane = lax.broadcasted_iota(jnp.int32, (PIECE, 128), 1)
    row = lax.broadcasted_iota(jnp.int32, (PIECE, 128), 0)
    freq = jnp.zeros((PIECE, 128), F32)
    for i, value in enumerate(FREQS):
        freq = jnp.where(lane % 32 == i, value, freq)
    tables = []
    for g in range(GROUPS):
        position = ctx * 512 + g * BLOCK + grp * PIECE + row
        angle = position.astype(F32) * freq
        cosine = jnp.where(lane < ROPE, jnp.cos(angle), 0.0)
        sine = jnp.where(lane < ROPE, jnp.sin(angle), 0.0)
        tables.append((cosine, jnp.where(lane < 32, -sine, sine)))

    loads["tok"].wait()
    loads["w"].wait()

    core_copies = []
    for g in range(GROUPS):
        product = dot_nt(tok_v[g * BLOCK : (g + 1) * BLOCK, :], w_v[...])
        for x in range(4):
            for c in range(2):
                at_row = (x * 2 + c) * PIECE
                part[g, c, x * PIECE : (x + 1) * PIECE, :] = product[at_row : at_row + PIECE]
        if g == 0:
            pl.semaphore_wait(barrier, len(peers))
        copy = remote(part.at[g, other], from_core.at[g], core_send.at[g], core_recv.at[g], sibling)
        copy.start()
        core_copies.append(copy)

    x_copies = []
    for g in range(GROUPS):
        core_copies[g].wait_recv()
        chip_sum[g] = part[g, core] + from_core[g]
        for i, delta in enumerate(DELTAS):
            to_x = lax.rem(at["x"] + delta, 4)
            copy = remote(
                chip_sum.at[g, pl.ds(pl.multiple_of(to_x * PIECE, PIECE), PIECE)],
                from_x.at[g, i],
                x_send.at[g * 3 + i],
                x_recv.at[g * 3 + i],
                moved("x", delta),
            )
            copy.start()
            x_copies.append(copy)

    sends = []

    def place(g, k):
        first, second = ORDERS[g][0][k], ORDERS[g][1][k]
        if first == second:
            return at[first]
        return jnp.where(core == 0, at[first], at[second])

    def toward(g, k, delta):
        first, second = ORDERS[g][0][k], ORDERS[g][1][k]
        new = dict(at)
        if first == second:
            new[first] = lax.rem(at[first] + delta, 4)
        else:
            new[first] = lax.rem(at[first] + delta * (1 - core), 4)
            new[second] = lax.rem(at[second] + delta * core, 4)
        return device(new["x"], new["y"], new["z"], core)

    def base(g, plane):
        return (plane * GROUPS + g) * GROUP_ROWS

    def rows_at(start, count):
        return buf.at[pl.ds(pl.multiple_of(start, PIECE), count)]

    def gather_send(g, slot, start, count, k, delta):
        copy = remote(
            rows_at(start, count),
            rows_at(start, count),
            g_send.at[g * 12 + slot],
            g_recv.at[g * 12 + slot],
            toward(g, k, delta),
        )
        copy.start()
        sends.append(copy)

    def gather_wait(g, slot, start, count):
        remote(
            rows_at(start, count),
            rows_at(start, count),
            g_send.at[g * 12 + slot],
            g_recv.at[g * 12 + slot],
            sibling,
        ).wait_recv()

    def pass_on(g, slot, start, count):
        copy = remote(
            rows_at(start, count), rows_at(start, count), f_send.at[g * 7 + slot], f_recv.at[g * 7 + slot], sibling
        )
        copy.start()
        sends.append(copy)

    spots = []
    for g in range(GROUPS):
        spots.append(tuple(place(g, k) for k in range(3)))

    def finish_sum(g):
        for i in range(3):
            x_copies[g * 3 + i].wait_recv()
        summed = (
            chip_sum[g, pl.ds(pl.multiple_of(at["x"] * PIECE, PIECE), PIECE), :]
            + from_x[g, 0]
            + from_x[g, 1]
            + from_x[g, 2]
        )
        latent = summed[:, :RANK]
        power = jnp.mean(latent * latent, axis=1, keepdims=True)
        normed = latent * lax.rsqrt(power + eps_norm) * gain[...]
        tail = summed[:, RANK:]
        pair = jnp.concatenate([tail, tail], axis=1)
        swapped = jnp.where(lane < 32, pltpu.roll(pair, 96, 1), pltpu.roll(pair, 32, 1))
        cosine, sine = tables[g]
        turned = pair * cosine + swapped * sine
        own = base(g, core) + spots[g][2] * 256 + spots[g][1] * 64 + spots[g][0] * 16
        here = pl.ds(pl.multiple_of(own, PIECE), PIECE)
        buf[here, :RANK] = normed.astype(BF16)
        buf[here, RANK:] = turned.astype(BF16)

    def phase1(g):
        own = base(g, core) + spots[g][2] * 256 + spots[g][1] * 64 + spots[g][0] * 16
        for i, delta in enumerate(DELTAS):
            gather_send(g, i, own, PIECE, 0, delta)

    def phase2(g):
        line = base(g, core) + spots[g][2] * 256 + spots[g][1] * 64
        for i, delta in enumerate(DELTAS):
            gather_wait(g, i, line + lax.rem(spots[g][0] + 4 - delta, 4) * 16, PIECE)
        for i, delta in enumerate(DELTAS):
            gather_send(g, 3 + i, line, 64, 1, delta)

    def half(g, offset, h):
        return base(g, core) + lax.rem(spots[g][2] + offset, 4) * 256 + h * 128

    def phase3(g):
        plane = base(g, core) + spots[g][2] * 256
        for i, delta in enumerate(DELTAS):
            gather_wait(g, 3 + i, plane + lax.rem(spots[g][1] + 4 - delta, 4) * 64, 64)
        gather_send(g, 6, half(g, 0, 0), 128, 2, 1)
        gather_send(g, 7, half(g, 0, 1), 128, 2, 3)
        gather_send(g, 8, half(g, 0, 1), 128, 2, 1)
        gather_send(g, 9, half(g, 0, 0), 128, 2, 3)
        pass_on(g, 0, plane, 256)

    def forward(g):
        gather_wait(g, 6, half(g, 3, 0), 128)
        gather_send(g, 10, half(g, 3, 0), 128, 2, 1)
        gather_wait(g, 7, half(g, 1, 1), 128)
        gather_send(g, 11, half(g, 1, 1), 128, 2, 3)
        pass_on(g, 1, half(g, 3, 0), 128)
        pass_on(g, 2, half(g, 1, 1), 128)

    def near(g):
        gather_wait(g, 8, half(g, 3, 1), 128)
        pass_on(g, 3, half(g, 3, 1), 128)
        gather_wait(g, 9, half(g, 1, 0), 128)
        pass_on(g, 4, half(g, 1, 0), 128)

    def far(g):
        gather_wait(g, 10, half(g, 2, 0), 128)
        pass_on(g, 5, half(g, 2, 0), 128)
        gather_wait(g, 11, half(g, 2, 1), 128)
        pass_on(g, 6, half(g, 2, 1), 128)

    def passed(g, slots):
        for slot in slots:
            count = 256 if slot == 0 else 128
            start = base(g, other)
            remote(
                rows_at(start, count), rows_at(start, count), f_send.at[g * 7 + slot], f_recv.at[g * 7 + slot], sibling
            ).wait_recv()

    def copy_window(g, slot, where):
        for x in range(4):
            for c in range(2):
                start = base(g, c)
                for axis, stride in zip(ORDERS[g][c], SLOT_STRIDE, strict=True):
                    start = start + (x if axis == "x" else where[axis]) * stride
                piece = buf[pl.ds(pl.multiple_of(start, PIECE), PIECE), :]
                target = slot * BLOCK + (x * 2 + c) * PIECE
                win[0, target : target + PIECE, :] = piece
                win[1, target : target + PIECE, :] = pltpu.roll(piece.astype(F32), 64, 1).astype(BF16)

    def prefill(b):
        first = ctx * 4 + b
        qrow = lax.rem(lax.broadcasted_iota(jnp.int32, (4 * BLOCK, 2 * BLOCK), 0), BLOCK)
        kcol = lax.broadcasted_iota(jnp.int32, (4 * BLOCK, 2 * BLOCK), 1)
        floor = jnp.where(first > 0, 0, BLOCK)
        allowed = (kcol >= floor) & (kcol - BLOCK <= qrow)
        values = win[0, b * BLOCK : (b + 2) * BLOCK, :RANK]

        def quad(j, carry):
            for odd in range(2):
                queries = jnp.concatenate(
                    [
                        q_v[
                            b * BLOCK : (b + 1) * BLOCK,
                            pl.ds(pl.multiple_of(j * (8 * WIDTH) + p * (2 * WIDTH) + odd * RANK, 128), WIDE),
                        ]
                        for p in range(4)
                    ],
                    axis=0,
                )
                scores = dot_nt(queries, win[odd, b * BLOCK : (b + 2) * BLOCK, :])
                scores = jnp.where(allowed, scores, neg_fill)
                peak = jnp.max(scores, axis=1, keepdims=True)
                expo = jnp.exp2((scores - peak) * EXP2_SCALE)
                share = 1.0 / jnp.sum(expo, axis=1, keepdims=True)
                weights = (expo * share).astype(BF16)
                latent = dot_nn(weights, values).astype(BF16)
                for p in range(4):
                    column = pl.ds(pl.multiple_of(j * 1024 + (2 * p + odd) * 128, 128), 128)
                    result = dot_nn(latent[p * BLOCK : (p + 1) * BLOCK], uv_v[:, column])
                    out_v[b * BLOCK : (b + 1) * BLOCK, column] = result.astype(BF16)
            return carry

        lax.fori_loop(0, 2, quad, 0)
        out = pltpu.make_async_copy(
            out_v.at[pl.ds(b * BLOCK, BLOCK)], o_pre.at[pl.ds(b * BLOCK, BLOCK)], out_sem.at[b]
        )
        out.start()
        return out

    def decode_start():
        loads["qd"].wait()
        loads["kv"].wait()
        wide = lax.broadcasted_iota(jnp.int32, (PIECE, WIDE), 1)
        for h in range(DEC_HEADS):
            for s in range(2):
                column = (h // 2) * (2 * WIDTH) + (h % 2) * RANK
                piece = qd_v[s, :, column : column + WIDE].astype(F32)
                if h % 2:
                    piece = pltpu.roll(piece, WIDE - 64, 1)
                piece = jnp.where(wide < WIDTH, piece, 0.0)
                qs[h * 32 + s * 16 : h * 32 + (s + 1) * 16, :] = piece.astype(BF16)
        kn[...] = jnp.zeros_like(kn)
        for t in range(2):
            kn[t * 16 : (t + 1) * 16, :WIDTH] = kv_v[t]
        rows = lax.broadcasted_iota(jnp.int32, (256, 32), 0)
        cols = lax.broadcasted_iota(jnp.int32, (256, 32), 1)
        allowed = (lax.rem(rows, 16) == lax.rem(cols, 16)) & (cols // 16 <= lax.rem(rows, 32) // 16)
        scores = jnp.where(allowed, dot_nt(qs[...], kn[...]), neg_fill)
        peak = jnp.max(scores, axis=1, keepdims=True)
        expo = jnp.exp2((scores - peak) * EXP2_SCALE)
        top[...] = jnp.broadcast_to(peak, (256, 128))
        total[...] = jnp.broadcast_to(jnp.sum(expo, axis=1, keepdims=True), (256, 128))
        acc[...] = dot_nn(expo.astype(BF16), kn[:, :RANK])

    request = lax.rem(lax.broadcasted_iota(jnp.int32, (256, 1), 0), 16)
    limit = jnp.zeros((256, 1), jnp.int32)
    for r in range(16):
        limit = jnp.where(request == r, lengths[r], limit)

    def decode_chunk(plane, g):
        start = base(g, plane)
        key = lax.broadcasted_iota(jnp.int32, (1, GROUP_ROWS), 1)
        position = g * BLOCK + plane * PIECE + lax.rem(key, PIECE)
        for axis, stride in zip(ORDERS[g][plane], SLOT_STRIDE, strict=True):
            position = position + lax.rem(key // stride, 4) * POS_STRIDE[axis]
        scores = dot_nt(qs[...], buf[start : start + GROUP_ROWS, :])
        scores = jnp.where(position < limit, scores, neg_fill)
        before = top[:, :1]
        peak = jnp.maximum(before, jnp.max(scores, axis=1, keepdims=True))
        factor = jnp.exp2((before - peak) * EXP2_SCALE)
        expo = jnp.exp2((scores - peak) * EXP2_SCALE)
        top[...] = jnp.broadcast_to(peak, (256, 128))
        total[...] = total[...] * factor + jnp.sum(expo, axis=1, keepdims=True)
        acc[...] = acc[...] * factor + dot_nn(expo.astype(BF16), buf[start : start + GROUP_ROWS, :RANK])

    def pick_pages(plane, g):
        for owner in range(16):
            target = owner * 32 + plane * PIECE
            piece = cache_v[target : target + PIECE, :] if g else jnp.zeros((PIECE, WIDTH), BF16)
            where = {"y": owner % 4, "z": owner // 4}
            for x in range(4):
                start = base(g, plane)
                for axis, stride in zip(ORDERS[g][plane], SLOT_STRIDE, strict=True):
                    start = start + (x if axis == "x" else where[axis]) * stride
                mine = block_map[owner * 16 + g * 4 + x] == ctx
                piece = jnp.where(mine, buf[start : start + PIECE, :WIDTH], piece)
            cache_v[target : target + PIECE, :] = piece

    def decode_end():
        result = (acc[...] / total[:, :1]).astype(BF16)
        for h in range(DEC_HEADS):
            for s in range(2):
                at_row = h * 32 + s * 16
                dec_v[s, :, h * RANK : (h + 1) * RANK] = result[at_row : at_row + 16]

    finish_sum(0)
    phase1(0)
    finish_sum(1)
    phase1(1)
    finish_sum(2)
    phase1(2)
    phase2(0)
    finish_sum(3)
    phase1(3)
    phase2(1)
    phase2(2)
    phase3(0)
    phase2(3)
    phase3(1)
    phase3(2)
    phase3(3)
    decode_start()
    loads["q"].wait()
    loads["uv"].wait()
    for g in range(GROUPS):
        passed(g, (0,))
    copy_window(1, 2, at)
    copy_window(2, 3, at)
    copy_window(3, 4, at)
    outs = []
    outs.append(prefill(2))
    for g in range(GROUPS):
        forward(g)
    outs.append(prefill(3))
    for g in range(GROUPS):
        near(g)
    for g in range(GROUPS):
        far(g)
    for g in range(GROUPS):
        passed(g, range(1, 7))
    copy_window(0, 1, at)
    behind = lax.rem(ctx + 15, 16)
    copy_window(3, 0, {"z": behind // 4, "y": lax.rem(behind, 4)})
    outs.append(prefill(1))
    outs.append(prefill(0))
    for plane in range(2):
        for g in range(GROUPS):
            decode_chunk(plane, g)
            pick_pages(plane, g)
    out = pltpu.make_async_copy(cache_v, o_cache, out_sem.at[4])
    out.start()
    outs.append(out)
    decode_end()
    out = pltpu.make_async_copy(dec_v, o_dec, out_sem.at[5])
    out.start()
    outs.append(out)
    for copy in core_copies + x_copies + sends:
        copy.wait_send()
    for out in outs:
        out.wait()


def shards(tokens, w_dkv, latent_gain, q_pre, w_uv, q_dec, kv_new, lengths, block_map):
    anywhere = pl.BlockSpec(memory_space=pl.ANY)
    vmem = pl.BlockSpec(memory_space=pltpu.VMEM)
    smem = pl.BlockSpec(memory_space=pltpu.SMEM)
    sems = pltpu.SemaphoreType.DMA
    return pl.pallas_call(
        kernel,
        out_shape=(
            jax.ShapeDtypeStruct((512, 2048), BF16),
            jax.ShapeDtypeStruct((512, WIDTH), BF16),
            jax.ShapeDtypeStruct((2, 16, 4096), BF16),
        ),
        in_specs=[anywhere, anywhere, vmem, anywhere, anywhere, anywhere, anywhere, smem, smem],
        out_specs=(anywhere, anywhere, anywhere),
        scratch_shapes=[
            pltpu.VMEM((512, 896), BF16),
            pltpu.VMEM((WIDTH, 896), BF16),
            pltpu.VMEM((512, HEADS * WIDTH), BF16),
            pltpu.VMEM((RANK, 2048), BF16),
            pltpu.VMEM((2, 16, DEC_HEADS * WIDTH), BF16),
            pltpu.VMEM((2, 16, WIDTH), BF16),
            pltpu.VMEM((GROUPS, 2, 64, WIDTH), F32),
            pltpu.VMEM((GROUPS, 64, WIDTH), F32),
            pltpu.VMEM((GROUPS, 64, WIDTH), F32),
            pltpu.VMEM((GROUPS, 3, PIECE, WIDTH), F32),
            pltpu.VMEM((2 * GROUPS * GROUP_ROWS, WIDE), BF16),
            pltpu.VMEM((2, 5 * BLOCK, WIDE), BF16),
            pltpu.VMEM((256, WIDE), BF16),
            pltpu.VMEM((32, WIDE), BF16),
            pltpu.VMEM((256, RANK), F32),
            pltpu.VMEM((256, 128), F32),
            pltpu.VMEM((256, 128), F32),
            pltpu.VMEM((512, 2048), BF16),
            pltpu.VMEM((512, WIDTH), BF16),
            pltpu.VMEM((2, 16, 4096), BF16),
            sems((6,)),
            sems((GROUPS,)),
            sems((GROUPS,)),
            sems((GROUPS * 3,)),
            sems((GROUPS * 3,)),
            sems((GROUPS * 12,)),
            sems((GROUPS * 12,)),
            sems((GROUPS * 7,)),
            sems((GROUPS * 7,)),
            sems((6,)),
        ],
        compiler_params=pltpu.CompilerParams(
            collective_id=0, has_side_effects=True, vmem_limit_bytes=56 * 1024 * 1024
        ),
    )(tokens, w_dkv.T, latent_gain.reshape(1, RANK), q_pre, w_uv, q_dec, kv_new, lengths, block_map)


def solution(mesh):
    placed = (
        P("ctx", "grp"),
        P("grp", None),
        P(),
        P("ctx", "grp"),
        P(None, "grp"),
        P(None, "grp", None),
        P(None, "grp", None),
        P("grp"),
        P(),
    )
    return jax.shard_map(
        shards,
        mesh=mesh,
        in_specs=placed,
        out_specs=(P("ctx", "grp"), P("ctx", None), P(None, "grp", "ctx")),
        check_vma=False,
    )
```

```python
import math

import jax
import jax.numpy as jnp
import numpy as np
from jax import lax
from jax.experimental import pallas as pl
from jax.experimental.pallas import tpu as pltpu
from jax.sharding import PartitionSpec as P

MESH = pl.DeviceIdType.MESH
F32 = jnp.float32
BF16 = jnp.bfloat16

scale_qk = 0.07216878364870322
eps_norm = 1e-06
neg_fill = -1e30
EXP2_SCALE = scale_qk * math.log2(math.e)

RANK = 512
WIDTH = 576
WIDE = 640
ROPE = 64
BLOCK = 128
PIECE = 16
GROUPS = 4
GROUP_ROWS = 1024
HEADS = 16
DEC_HEADS = 8

ORDERS = (
    ("yzx", "zyx"),
    ("zxy", "xzy"),
    ("yxz", "xyz"),
    ("xzy", "xyz"),
)
ROW_BLOCK = (3, 0, 1, 2)
POS_STRIDE = {"z": 2048, "y": 512, "x": 32}
SLOT_STRIDE = (PIECE, 4 * PIECE, 16 * PIECE)
DELTAS = (1, 3, 2)
FREQS = [float(np.float32(10000.0 ** (-2.0 * i / ROPE))) for i in range(ROPE // 2)]


def dot_nt(a, b):
    return lax.dot_general(a, b, (((1,), (1,)), ((), ())), preferred_element_type=F32)


def dot_nn(a, b):
    return jnp.dot(a, b, preferred_element_type=F32)


def base(g, plane):
    return (plane * GROUPS + g) * GROUP_ROWS


def attend(parts, at, lengths, buf, qs, acc, top, total):
    request = lax.rem(lax.broadcasted_iota(jnp.int32, (256, 1), 0), 16)
    limit = jnp.zeros((256, 1), jnp.int32)
    for r in range(16):
        limit = jnp.where(request == r, lengths[r], limit)
    spans, masks = [], []
    for plane, g, offset in parts:
        order = ORDERS[g][plane]
        count = GROUP_ROWS if offset is None else 256
        last = 0 if offset is None else lax.rem(at[order[2]] + offset, 4)
        spans.append(pl.ds(pl.multiple_of(base(g, plane) + last * 256, 256), count))
        key = lax.broadcasted_iota(jnp.int32, (1, count), 1)
        position = ROW_BLOCK[g] * BLOCK + plane * PIECE + lax.rem(key, PIECE) + last * POS_STRIDE[order[2]]
        for axis, stride in zip(order, SLOT_STRIDE, strict=True):
            position = position + lax.rem(key // stride, 4) * POS_STRIDE[axis]
        masks.append(position < limit)
    keys = jnp.concatenate([buf[span, :] for span in spans], axis=0)
    scores = dot_nt(qs[...], keys)
    scores = jnp.where(jnp.concatenate(masks, axis=1), scores, neg_fill)
    before = top[:, :1]
    peak = jnp.maximum(before, jnp.max(scores, axis=1, keepdims=True))
    factor = jnp.exp2((before - peak) * EXP2_SCALE)
    expo = jnp.exp2((scores - peak) * EXP2_SCALE)
    top[...] = jnp.broadcast_to(peak, (256, 128))
    total[...] = total[...] * factor + jnp.sum(expo, axis=1, keepdims=True)
    values = jnp.concatenate([buf[span, :RANK] for span in spans], axis=0)
    acc[...] = acc[...] * factor + dot_nn(expo.astype(BF16), values)


def kernel(
    tokens,
    w_dkv,
    gain,
    q_pre,
    w_uv,
    q_dec,
    kv_new,
    lengths,
    o_pre,
    buf,
    qs,
    acc,
    top,
    total,
    tok_v,
    w_v,
    q_v,
    uv_v,
    qd_v,
    kv_v,
    part,
    from_core,
    chip_sum,
    from_x,
    win,
    kn,
    pre_s,
    pre_w,
    load_sem,
    core_send,
    core_recv,
    x_send,
    x_recv,
    g_send,
    g_recv,
    f_send,
    f_recv,
    l_send,
    l_recv,
):
    ctx = lax.axis_index("ctx")
    grp = lax.axis_index("grp")
    at = {"z": ctx // 4, "y": lax.rem(ctx, 4), "x": grp // 2}
    core = lax.rem(grp, 2)
    other = 1 - core

    def device(x, y, z, c):
        return (z * 4 + y, x * 2 + c)

    def moved(axis, delta):
        new = dict(at)
        new[axis] = lax.rem(at[axis] + delta, 4)
        return device(new["x"], new["y"], new["z"], core)

    sibling = device(at["x"], at["y"], at["z"], other)

    loads = {
        "tok": pltpu.make_async_copy(tokens, tok_v, load_sem.at[0]),
        "w": pltpu.make_async_copy(w_dkv, w_v, load_sem.at[1]),
        "qd": pltpu.make_async_copy(
            q_dec.at[:, :, pl.ds(pl.multiple_of(ctx * (DEC_HEADS * WIDTH), 128), DEC_HEADS * WIDTH)],
            qd_v,
            load_sem.at[2],
        ),
        "kv": pltpu.make_async_copy(kv_new, kv_v, load_sem.at[3]),
        "q": pltpu.make_async_copy(q_pre, q_v, load_sem.at[4]),
        "uv": pltpu.make_async_copy(w_uv, uv_v, load_sem.at[5]),
    }
    loads["tok"].start()
    loads["w"].start()

    barrier = pltpu.get_barrier_semaphore()
    across = [device(lax.rem(at["x"] + delta, 4), at["y"], at["z"], other) for delta in DELTAS]
    peers = [sibling] + across + [moved(axis, delta) for axis in "xyz" for delta in DELTAS]
    for peer in peers:
        pl.semaphore_signal(barrier, inc=1, device_id=peer, device_id_type=MESH)

    def remote(src, dst, send, recv, to):
        return pltpu.make_async_remote_copy(
            src_ref=src, dst_ref=dst, send_sem=send, recv_sem=recv, device_id=to, device_id_type=MESH
        )

    lane = lax.broadcasted_iota(jnp.int32, (PIECE, 128), 1)
    row = lax.broadcasted_iota(jnp.int32, (PIECE, 128), 0)
    freq = jnp.zeros((PIECE, 128), F32)
    for i, value in enumerate(FREQS):
        freq = jnp.where(lane % 32 == i, value, freq)
    tables = []
    for g in range(GROUPS):
        position = ctx * 512 + ROW_BLOCK[g] * BLOCK + grp * PIECE + row
        angle = position.astype(F32) * freq
        cosine = jnp.where(lane < ROPE, jnp.cos(angle), 0.0)
        sine = jnp.where(lane < ROPE, jnp.sin(angle), 0.0)
        tables.append((cosine, jnp.where(lane < 32, -sine, sine)))

    loads["tok"].wait()
    loads["w"].wait()
    for name in ("qd", "kv", "q", "uv"):
        loads[name].start()

    core_copies = []
    x_copies = []

    def project(g):
        first = ROW_BLOCK[g] * BLOCK
        product = dot_nt(tok_v[first : first + BLOCK, :], w_v[...])
        for x in range(4):
            for c in range(2):
                at_row = (x * 2 + c) * PIECE
                part[g, c, x * PIECE : (x + 1) * PIECE, :] = product[at_row : at_row + PIECE]

    def to_core(g):
        copy = remote(part.at[g, other], from_core.at[g], core_send.at[g], core_recv.at[g], sibling)
        copy.start()
        core_copies.append(copy)

    def to_x(g):
        core_copies[g].wait_recv()
        chip_sum[g] = part[g, core] + from_core[g]
        for i, delta in enumerate(DELTAS):
            target = lax.rem(at["x"] + delta, 4)
            copy = remote(
                chip_sum.at[g, pl.ds(pl.multiple_of(target * PIECE, PIECE), PIECE)],
                from_x.at[g, i],
                x_send.at[g * 3 + i],
                x_recv.at[g * 3 + i],
                moved("x", delta),
            )
            copy.start()
            x_copies.append(copy)

    project(0)
    pl.semaphore_wait(barrier, len(peers))
    to_core(0)
    project(1)
    to_core(1)
    project(2)
    to_core(2)
    to_x(0)
    project(3)
    to_core(3)
    for g in range(1, GROUPS):
        to_x(g)

    sends = []

    def place(g, k):
        first, second = ORDERS[g][0][k], ORDERS[g][1][k]
        if first == second:
            return at[first]
        return jnp.where(core == 0, at[first], at[second])

    def toward(g, k, delta):
        first, second = ORDERS[g][0][k], ORDERS[g][1][k]
        new = dict(at)
        if first == second:
            new[first] = lax.rem(at[first] + delta, 4)
        else:
            new[first] = lax.rem(at[first] + delta * (1 - core), 4)
            new[second] = lax.rem(at[second] + delta * core, 4)
        return device(new["x"], new["y"], new["z"], core)

    def rows_at(start, count):
        return buf.at[pl.ds(pl.multiple_of(start, PIECE), count)]

    def gather_send(g, slot, start, count, k, delta):
        copy = remote(
            rows_at(start, count),
            rows_at(start, count),
            g_send.at[g * 12 + slot],
            g_recv.at[g * 12 + slot],
            toward(g, k, delta),
        )
        copy.start()
        sends.append(copy)

    def gather_wait(g, slot, start, count):
        remote(
            rows_at(start, count),
            rows_at(start, count),
            g_send.at[g * 12 + slot],
            g_recv.at[g * 12 + slot],
            sibling,
        ).wait_recv()

    def pass_on(g, slot, start, count):
        copy = remote(
            rows_at(start, count), rows_at(start, count), f_send.at[g * 7 + slot], f_recv.at[g * 7 + slot], sibling
        )
        copy.start()
        sends.append(copy)

    spots = []
    for g in range(GROUPS):
        spots.append(tuple(place(g, k) for k in range(3)))

    def finish_sum(g):
        for i in range(3):
            x_copies[g * 3 + i].wait_recv()
        summed = (
            chip_sum[g, pl.ds(pl.multiple_of(at["x"] * PIECE, PIECE), PIECE), :]
            + from_x[g, 0]
            + from_x[g, 1]
            + from_x[g, 2]
        )
        latent = summed[:, :RANK]
        power = jnp.mean(latent * latent, axis=1, keepdims=True)
        normed = latent * lax.rsqrt(power + eps_norm) * gain[...]
        tail = summed[:, RANK:]
        pair = jnp.concatenate([tail, tail], axis=1)
        swapped = jnp.where(lane < 32, pltpu.roll(pair, 96, 1), pltpu.roll(pair, 32, 1))
        cosine, sine = tables[g]
        turned = pair * cosine + swapped * sine
        own = base(g, core) + spots[g][2] * 256 + spots[g][1] * 64 + spots[g][0] * 16
        here = pl.ds(pl.multiple_of(own, PIECE), PIECE)
        buf[here, :RANK] = normed.astype(BF16)
        buf[here, RANK:] = turned.astype(BF16)

    def phase1(g):
        own = base(g, core) + spots[g][2] * 256 + spots[g][1] * 64 + spots[g][0] * 16
        for i, delta in enumerate(DELTAS):
            gather_send(g, i, own, PIECE, 0, delta)

    def line_at(x, c):
        return win.at[0, pl.ds(pl.multiple_of(4 * BLOCK + (x * 2 + c) * PIECE, PIECE), PIECE)]

    line_to = [moved("x", delta) for delta in DELTAS] + across + [sibling]

    def send_line():
        own = base(0, core) + spots[0][2] * 256 + spots[0][1] * 64 + spots[0][0] * 16
        for i, to in enumerate(line_to):
            copy = remote(rows_at(own, PIECE), line_at(at["x"], core), l_send.at[i], l_recv.at[i], to)
            copy.start()
            sends.append(copy)
        win[0, pl.ds(pl.multiple_of(4 * BLOCK + grp * PIECE, PIECE), PIECE), :] = buf[
            pl.ds(pl.multiple_of(own, PIECE), PIECE), :
        ]

    def wait_line():
        own = base(0, core) + spots[0][2] * 256 + spots[0][1] * 64 + spots[0][0] * 16
        for i in range(len(line_to)):
            x = at["x"] if i == 6 else lax.rem(at["x"] + 4 - DELTAS[i % 3], 4)
            c = core if i < 3 else other
            remote(rows_at(own, PIECE), line_at(x, c), l_send.at[i], l_recv.at[i], sibling).wait_recv()
        for k in range(8):
            target = 4 * BLOCK + k * PIECE
            piece = win[0, target : target + PIECE, :]
            win[1, target : target + PIECE, :] = pltpu.roll(piece.astype(F32), 64, 1).astype(BF16)

    def phase2(g):
        line = base(g, core) + spots[g][2] * 256 + spots[g][1] * 64
        for i, delta in enumerate(DELTAS):
            gather_wait(g, i, line + lax.rem(spots[g][0] + 4 - delta, 4) * 16, PIECE)
        for i, delta in enumerate(DELTAS):
            gather_send(g, 3 + i, line, 64, 1, delta)

    def half(g, offset, h):
        return base(g, core) + lax.rem(spots[g][2] + offset, 4) * 256 + h * 128

    def phase3(g):
        plane = base(g, core) + spots[g][2] * 256
        for i, delta in enumerate(DELTAS):
            gather_wait(g, 3 + i, plane + lax.rem(spots[g][1] + 4 - delta, 4) * 64, 64)
        gather_send(g, 6, half(g, 0, 0), 128, 2, 1)
        gather_send(g, 7, half(g, 0, 1), 128, 2, 3)
        gather_send(g, 8, half(g, 0, 1), 128, 2, 1)
        gather_send(g, 9, half(g, 0, 0), 128, 2, 3)
        pass_on(g, 0, plane, 256)

    def forward(g):
        gather_wait(g, 6, half(g, 3, 0), 128)
        gather_send(g, 10, half(g, 3, 0), 128, 2, 1)
        gather_wait(g, 7, half(g, 1, 1), 128)
        gather_send(g, 11, half(g, 1, 1), 128, 2, 3)
        pass_on(g, 1, half(g, 3, 0), 128)
        pass_on(g, 2, half(g, 1, 1), 128)

    def near(g):
        gather_wait(g, 8, half(g, 3, 1), 128)
        pass_on(g, 3, half(g, 3, 1), 128)
        gather_wait(g, 9, half(g, 1, 0), 128)
        pass_on(g, 4, half(g, 1, 0), 128)

    def far(g):
        gather_wait(g, 10, half(g, 2, 0), 128)
        pass_on(g, 5, half(g, 2, 0), 128)
        gather_wait(g, 11, half(g, 2, 1), 128)
        pass_on(g, 6, half(g, 2, 1), 128)

    def passed(g, slots):
        for slot in slots:
            count = 256 if slot == 0 else 128
            start = base(g, other)
            remote(
                rows_at(start, count), rows_at(start, count), f_send.at[g * 7 + slot], f_recv.at[g * 7 + slot], sibling
            ).wait_recv()

    def copy_window(g, slot, where):
        for x in range(4):
            for c in range(2):
                start = base(g, c)
                for axis, stride in zip(ORDERS[g][c], SLOT_STRIDE, strict=True):
                    start = start + (x if axis == "x" else where[axis]) * stride
                piece = buf[pl.ds(pl.multiple_of(start, PIECE), PIECE), :]
                target = slot * BLOCK + (x * 2 + c) * PIECE
                win[0, target : target + PIECE, :] = piece
                win[1, target : target + PIECE, :] = pltpu.roll(piece.astype(F32), 64, 1).astype(BF16)

    def prefill(b):
        first = ctx * 4 + b
        qrow = lax.broadcasted_iota(jnp.int32, (BLOCK, 2 * BLOCK), 0)
        kcol = lax.broadcasted_iota(jnp.int32, (BLOCK, 2 * BLOCK), 1)
        floor = jnp.where(first > 0, 0, BLOCK)
        allowed = (kcol >= floor) & (kcol - BLOCK <= qrow)
        mine = slice(b * BLOCK, (b + 1) * BLOCK)
        for odd in range(2):
            queries = jnp.concatenate(
                [q_v[mine, p * 2 * WIDTH + odd * RANK : p * 2 * WIDTH + odd * RANK + WIDE] for p in range(8)], axis=0
            )
            pre_s[odd] = dot_nt(queries, win[odd, b * BLOCK : (b + 2) * BLOCK, :])
        for odd in range(2):
            for p in range(8):
                rows = slice(p * BLOCK, (p + 1) * BLOCK)
                scores = jnp.where(allowed, pre_s[odd, rows], neg_fill)
                peak = jnp.max(scores, axis=1, keepdims=True)
                expo = jnp.exp2((scores - peak) * EXP2_SCALE)
                share = 1.0 / jnp.sum(expo, axis=1, keepdims=True)
                pre_w[odd, rows] = (expo * share).astype(BF16)
        values = win[0, b * BLOCK : (b + 2) * BLOCK, :RANK]
        for odd in range(2):
            latent = dot_nn(pre_w[odd], values).astype(BF16)
            for p in range(8):
                column = slice((2 * p + odd) * 128, (2 * p + odd + 1) * 128)
                result = dot_nn(latent[p * BLOCK : (p + 1) * BLOCK], uv_v[:, column])
                o_pre[mine, column] = result.astype(BF16)

    def decode_start():
        loads["qd"].wait()
        loads["kv"].wait()
        wide = lax.broadcasted_iota(jnp.int32, (PIECE, WIDE), 1)
        for h in range(DEC_HEADS):
            for s in range(2):
                column = (h // 2) * (2 * WIDTH) + (h % 2) * RANK
                piece = qd_v[s, :, column : column + WIDE].astype(F32)
                if h % 2:
                    piece = pltpu.roll(piece, WIDE - 64, 1)
                piece = jnp.where(wide < WIDTH, piece, 0.0)
                qs[h * 32 + s * 16 : h * 32 + (s + 1) * 16, :] = piece.astype(BF16)
        kn[...] = jnp.zeros_like(kn)
        for t in range(2):
            kn[t * 16 : (t + 1) * 16, :WIDTH] = kv_v[t]
        rows = lax.broadcasted_iota(jnp.int32, (256, 32), 0)
        cols = lax.broadcasted_iota(jnp.int32, (256, 32), 1)
        allowed = (lax.rem(rows, 16) == lax.rem(cols, 16)) & (cols // 16 <= lax.rem(rows, 32) // 16)
        scores = jnp.where(allowed, dot_nt(qs[...], kn[...]), neg_fill)
        peak = jnp.max(scores, axis=1, keepdims=True)
        expo = jnp.exp2((scores - peak) * EXP2_SCALE)
        top[...] = jnp.broadcast_to(peak, (256, 128))
        total[...] = jnp.broadcast_to(jnp.sum(expo, axis=1, keepdims=True), (256, 128))
        acc[...] = dot_nn(expo.astype(BF16), kn[:, :RANK])

    def decode(parts):
        attend(parts, at, lengths, buf, qs, acc, top, total)

    finish_sum(0)
    phase1(0)
    send_line()
    finish_sum(1)
    phase1(1)
    finish_sum(2)
    phase1(2)
    phase2(0)
    finish_sum(3)
    phase1(3)
    phase2(1)
    phase2(2)
    phase3(0)
    phase2(3)
    phase3(1)
    phase3(2)
    phase3(3)
    decode_start()
    forward(0)
    loads["q"].wait()
    loads["uv"].wait()
    wait_line()
    for g in range(GROUPS):
        passed(g, (0,))
    for g in range(1, GROUPS):
        copy_window(g, g, at)
    prefill(1)
    forward(1)
    forward(2)
    near(0)
    prefill(2)
    forward(3)
    far(0)
    prefill(3)
    near(1)
    near(2)
    passed(0, range(1, 7))
    behind = lax.rem(ctx + 15, 16)
    copy_window(0, 0, {"z": behind // 4, "y": lax.rem(behind, 4)})
    decode([(0, 0, None)])
    decode([(1, 0, None)])
    far(1)
    far(2)
    prefill(0)
    near(3)
    passed(1, range(1, 7))
    decode([(0, 1, None)])
    decode([(1, 1, None)])
    passed(2, range(1, 7))
    far(3)
    decode([(0, 2, None)])
    decode([(1, 2, None)])
    passed(3, range(1, 5))
    decode([(c, 3, offset) for c in range(2) for offset in (0, 1, 3)])
    passed(3, range(5, 7))
    for copy in core_copies + x_copies + sends:
        copy.wait_send()


def finish(
    pre, buf, qs, acc_in, top_in, total_in, lengths, block_map, o_pre, o_cache, o_dec, acc, top, total, cache, flipped, dec, sems
):
    ctx = lax.axis_index("ctx")
    at = {"z": ctx // 4, "y": lax.rem(ctx, 4), "x": lax.axis_index("grp") // 2}
    pre_copy = pltpu.make_async_copy(pre, o_pre, sems.at[0])
    pre_copy.start()
    acc[...] = acc_in[...]
    top[...] = top_in[...]
    total[...] = total_in[...]
    attend([(0, 3, 2), (1, 3, 2)], at, lengths, buf, qs, acc, top, total)
    result = (acc[...] / total[:, :1]).astype(BF16)
    for h in range(DEC_HEADS):
        for s in range(2):
            at_row = h * 32 + s * 16
            dec[s, :, h * RANK : (h + 1) * RANK] = result[at_row : at_row + 16]
    dec_copy = pltpu.make_async_copy(dec, o_dec, sems.at[1])
    dec_copy.start()

    def take_page(owner, carry):
        def look(j, found):
            return jnp.where(block_map[owner * 16 + j] == ctx, j, found)

        page = lax.fori_loop(0, 16, look, jnp.int32(0), unroll=True)
        row_block = page // 4
        where = {"x": lax.rem(page, 4), "y": lax.rem(owner, 4), "z": owner // 4}
        for c in range(2):
            start = jnp.int32(0)
            for k in range(GROUPS):
                here = base(k, c)
                for axis, stride in zip(ORDERS[k][c], SLOT_STRIDE, strict=True):
                    here = here + where[axis] * stride
                start = jnp.where(row_block == ROW_BLOCK[k], here, start)
            target = pl.multiple_of(owner * 32 + c * PIECE, PIECE)
            cache[pl.ds(target, PIECE), :] = buf[pl.ds(pl.multiple_of(start, PIECE), PIECE), :]
        return carry

    lax.fori_loop(0, 16, take_page, 0)
    flipped[...] = cache[...].T[:WIDTH]
    cache_copy = pltpu.make_async_copy(flipped, o_cache, sems.at[2])
    cache_copy.start()
    for copy in (pre_copy, dec_copy, cache_copy):
        copy.wait()


def shards(tokens, w_dkv, latent_gain, q_pre, w_uv, q_dec, kv_new, lengths, block_map):
    anywhere = pl.BlockSpec(memory_space=pl.ANY)
    vmem = pl.BlockSpec(memory_space=pltpu.VMEM)
    smem = pl.BlockSpec(memory_space=pltpu.SMEM)
    sems = pltpu.SemaphoreType.DMA
    results = pl.pallas_call(
        kernel,
        out_shape=(
            pltpu.VMEM((512, 2048), BF16),
            pltpu.VMEM((2 * GROUPS * GROUP_ROWS, WIDE), BF16),
            pltpu.VMEM((256, WIDE), BF16),
            pltpu.VMEM((256, RANK), F32),
            pltpu.VMEM((256, 128), F32),
            pltpu.VMEM((256, 128), F32),
        ),
        in_specs=[anywhere, anywhere, vmem, anywhere, anywhere, anywhere, anywhere, smem],
        out_specs=(vmem,) * 6,
        scratch_shapes=[
            pltpu.VMEM((512, 896), BF16),
            pltpu.VMEM((WIDTH, 896), BF16),
            pltpu.VMEM((512, HEADS * WIDTH), BF16),
            pltpu.VMEM((RANK, 2048), BF16),
            pltpu.VMEM((2, 16, DEC_HEADS * WIDTH), BF16),
            pltpu.VMEM((2, 16, WIDTH), BF16),
            pltpu.VMEM((GROUPS, 2, 64, WIDTH), F32),
            pltpu.VMEM((GROUPS, 64, WIDTH), F32),
            pltpu.VMEM((GROUPS, 64, WIDTH), F32),
            pltpu.VMEM((GROUPS, 3, PIECE, WIDTH), F32),
            pltpu.VMEM((2, 5 * BLOCK, WIDE), BF16),
            pltpu.VMEM((32, WIDE), BF16),
            pltpu.VMEM((2, 1024, 256), F32),
            pltpu.VMEM((2, 1024, 256), BF16),
            sems((6,)),
            sems((GROUPS,)),
            sems((GROUPS,)),
            sems((GROUPS * 3,)),
            sems((GROUPS * 3,)),
            sems((GROUPS * 12,)),
            sems((GROUPS * 12,)),
            sems((GROUPS * 7,)),
            sems((GROUPS * 7,)),
            sems((7,)),
            sems((7,)),
        ],
        compiler_params=pltpu.CompilerParams(
            collective_id=0, has_side_effects=True, vmem_limit_bytes=48 * 1024 * 1024
        ),
    )(tokens, w_dkv.T, latent_gain.reshape(1, RANK), q_pre, w_uv, q_dec, kv_new, lengths)
    pre, cache, dec = pl.pallas_call(
        finish,
        out_shape=(
            jax.ShapeDtypeStruct((512, 2048), BF16),
            jax.ShapeDtypeStruct((WIDTH, 512), BF16),
            jax.ShapeDtypeStruct((2, 16, 4096), BF16),
        ),
        in_specs=[vmem] * 6 + [smem, smem],
        out_specs=(anywhere, anywhere, anywhere),
        scratch_shapes=[
            pltpu.VMEM((256, RANK), F32),
            pltpu.VMEM((256, 128), F32),
            pltpu.VMEM((256, 128), F32),
            pltpu.VMEM((512, WIDE), BF16),
            pltpu.VMEM((WIDTH, 512), BF16),
            pltpu.VMEM((2, 16, 4096), BF16),
            sems((3,)),
        ],
        compiler_params=pltpu.CompilerParams(vmem_limit_bytes=24 * 1024 * 1024),
    )(*results, lengths, block_map)
    return pre, cache.T, dec


def solution(mesh):
    placed = (
        P("ctx", "grp"),
        P("grp", None),
        P(),
        P("ctx", "grp"),
        P(None, "grp"),
        P(None, "grp", None),
        P(None, "grp", None),
        P("grp"),
        P(),
    )
    return jax.shard_map(
        shards,
        mesh=mesh,
        in_specs=placed,
        out_specs=(P("ctx", "grp"), P("ctx", None), P(None, "grp", "ctx")),
        check_vma=False,
    )
```

```python
import math

import jax
import jax.numpy as jnp
import numpy as np
from jax import lax
from jax.experimental import pallas as pl
from jax.experimental.pallas import tpu as pltpu
from jax.sharding import PartitionSpec as P

MESH = pl.DeviceIdType.MESH
F32 = jnp.float32
BF16 = jnp.bfloat16

scale_qk = 0.07216878364870322
eps_norm = 1e-06
neg_fill = -1e30
EXP2_SCALE = scale_qk * math.log2(math.e)

RANK = 512
WIDTH = 576
WIDE = 640
ROPE = 64
BLOCK = 128
PIECE = 16
GROUPS = 4
GROUP_ROWS = 1024
HEADS = 16
DEC_HEADS = 8

ORDERS = (
    ("yzx", "zyx"),
    ("zxy", "xzy"),
    ("yxz", "xyz"),
    ("xzy", "xyz"),
)
ROW_BLOCK = (3, 0, 1, 2)
POS_STRIDE = {"z": 2048, "y": 512, "x": 32}
SLOT_STRIDE = (PIECE, 4 * PIECE, 16 * PIECE)
DELTAS = (1, 3, 2)
FREQS = [float(np.float32(10000.0 ** (-2.0 * i / ROPE))) for i in range(ROPE // 2)]


def dot_nt(a, b):
    return lax.dot_general(a, b, (((1,), (1,)), ((), ())), preferred_element_type=F32)


def dot_nn(a, b):
    return jnp.dot(a, b, preferred_element_type=F32)


def base(g, plane):
    return (plane * GROUPS + g) * GROUP_ROWS


def attend(parts, at, lengths, buf, qs, acc, top, total):
    request = lax.rem(lax.broadcasted_iota(jnp.int32, (256, 1), 0), 16)
    limit = jnp.zeros((256, 1), jnp.int32)
    for r in range(16):
        limit = jnp.where(request == r, lengths[r], limit)
    spans, masks = [], []
    for plane, g, offset in parts:
        order = ORDERS[g][plane]
        count = GROUP_ROWS if offset is None else 256
        last = 0 if offset is None else lax.rem(at[order[2]] + offset, 4)
        spans.append(pl.ds(pl.multiple_of(base(g, plane) + last * 256, 256), count))
        key = lax.broadcasted_iota(jnp.int32, (1, count), 1)
        position = ROW_BLOCK[g] * BLOCK + plane * PIECE + lax.rem(key, PIECE) + last * POS_STRIDE[order[2]]
        for axis, stride in zip(order, SLOT_STRIDE, strict=True):
            position = position + lax.rem(key // stride, 4) * POS_STRIDE[axis]
        masks.append(position < limit)
    keys = jnp.concatenate([buf[span, :] for span in spans], axis=0)
    scores = dot_nt(qs[...], keys)
    scores = jnp.where(jnp.concatenate(masks, axis=1), scores, neg_fill)
    before = top[:, :1]
    peak = jnp.maximum(before, jnp.max(scores, axis=1, keepdims=True))
    factor = jnp.exp2((before - peak) * EXP2_SCALE)
    expo = jnp.exp2((scores - peak) * EXP2_SCALE)
    top[...] = jnp.broadcast_to(peak, (256, 128))
    total[...] = total[...] * factor + jnp.sum(expo, axis=1, keepdims=True)
    values = jnp.concatenate([buf[span, :RANK] for span in spans], axis=0)
    acc[...] = acc[...] * factor + dot_nn(expo.astype(BF16), values)


def kernel(
    tokens,
    w_dkv,
    gain,
    q_pre,
    w_uv,
    q_dec,
    kv_new,
    lengths,
    o_pre,
    buf,
    qs,
    acc,
    top,
    total,
    tok_v,
    w_v,
    q_v,
    uv_v,
    qd_v,
    kv_v,
    part,
    from_core,
    chip_sum,
    from_x,
    win,
    kn,
    pre_s,
    pre_w,
    load_sem,
    core_send,
    core_recv,
    x_send,
    x_recv,
    g_send,
    g_recv,
    f_send,
    f_recv,
    l_send,
    l_recv,
):
    ctx = lax.axis_index("ctx")
    grp = lax.axis_index("grp")
    at = {"z": ctx // 4, "y": lax.rem(ctx, 4), "x": grp // 2}
    core = lax.rem(grp, 2)
    other = 1 - core

    def device(x, y, z, c):
        return (z * 4 + y, x * 2 + c)

    def moved(axis, delta):
        new = dict(at)
        new[axis] = lax.rem(at[axis] + delta, 4)
        return device(new["x"], new["y"], new["z"], core)

    sibling = device(at["x"], at["y"], at["z"], other)

    loads = {
        "tok": pltpu.make_async_copy(tokens, tok_v, load_sem.at[0]),
        "w": pltpu.make_async_copy(w_dkv, w_v, load_sem.at[1]),
        "qd": pltpu.make_async_copy(
            q_dec.at[:, :, pl.ds(pl.multiple_of(ctx * (DEC_HEADS * WIDTH), 128), DEC_HEADS * WIDTH)],
            qd_v,
            load_sem.at[2],
        ),
        "kv": pltpu.make_async_copy(kv_new, kv_v, load_sem.at[3]),
        "q": pltpu.make_async_copy(q_pre, q_v, load_sem.at[4]),
        "uv": pltpu.make_async_copy(w_uv, uv_v, load_sem.at[5]),
    }
    loads["tok"].start()
    loads["w"].start()

    barrier = pltpu.get_barrier_semaphore()
    across = [device(lax.rem(at["x"] + delta, 4), at["y"], at["z"], other) for delta in DELTAS]
    peers = [sibling] + across + [moved(axis, delta) for axis in "xyz" for delta in DELTAS]
    for peer in peers:
        pl.semaphore_signal(barrier, inc=1, device_id=peer, device_id_type=MESH)

    def remote(src, dst, send, recv, to):
        return pltpu.make_async_remote_copy(
            src_ref=src, dst_ref=dst, send_sem=send, recv_sem=recv, device_id=to, device_id_type=MESH
        )

    lane = lax.broadcasted_iota(jnp.int32, (PIECE, 128), 1)
    row = lax.broadcasted_iota(jnp.int32, (PIECE, 128), 0)
    freq = jnp.zeros((PIECE, 128), F32)
    for i, value in enumerate(FREQS):
        freq = jnp.where(lane % 32 == i, value, freq)
    tables = []
    for g in range(GROUPS):
        position = ctx * 512 + ROW_BLOCK[g] * BLOCK + grp * PIECE + row
        angle = position.astype(F32) * freq
        cosine = jnp.where(lane < ROPE, jnp.cos(angle), 0.0)
        sine = jnp.where(lane < ROPE, jnp.sin(angle), 0.0)
        tables.append((cosine, jnp.where(lane < 32, -sine, sine)))

    loads["tok"].wait()
    loads["w"].wait()
    for name in ("qd", "kv", "q", "uv"):
        loads[name].start()

    core_copies = []
    x_copies = []

    def project(g):
        first = ROW_BLOCK[g] * BLOCK
        product = dot_nt(tok_v[first : first + BLOCK, :], w_v[...])
        for x in range(4):
            for c in range(2):
                at_row = (x * 2 + c) * PIECE
                part[g, c, x * PIECE : (x + 1) * PIECE, :] = product[at_row : at_row + PIECE]

    def to_core(g):
        copy = remote(part.at[g, other], from_core.at[g], core_send.at[g], core_recv.at[g], sibling)
        copy.start()
        core_copies.append(copy)

    def to_x(g):
        core_copies[g].wait_recv()
        chip_sum[g] = part[g, core] + from_core[g]
        for i, delta in enumerate(DELTAS):
            target = lax.rem(at["x"] + delta, 4)
            copy = remote(
                chip_sum.at[g, pl.ds(pl.multiple_of(target * PIECE, PIECE), PIECE)],
                from_x.at[g, i],
                x_send.at[g * 3 + i],
                x_recv.at[g * 3 + i],
                moved("x", delta),
            )
            copy.start()
            x_copies.append(copy)

    project(0)
    pl.semaphore_wait(barrier, len(peers))
    to_core(0)
    project(1)
    to_core(1)
    project(2)
    to_core(2)
    to_x(0)
    project(3)
    to_core(3)
    for g in range(1, GROUPS):
        to_x(g)

    sends = []

    def place(g, k):
        first, second = ORDERS[g][0][k], ORDERS[g][1][k]
        if first == second:
            return at[first]
        return jnp.where(core == 0, at[first], at[second])

    def toward(g, k, delta):
        first, second = ORDERS[g][0][k], ORDERS[g][1][k]
        new = dict(at)
        if first == second:
            new[first] = lax.rem(at[first] + delta, 4)
        else:
            new[first] = lax.rem(at[first] + delta * (1 - core), 4)
            new[second] = lax.rem(at[second] + delta * core, 4)
        return device(new["x"], new["y"], new["z"], core)

    def rows_at(start, count):
        return buf.at[pl.ds(pl.multiple_of(start, PIECE), count)]

    def gather_send(g, slot, start, count, k, delta):
        copy = remote(
            rows_at(start, count),
            rows_at(start, count),
            g_send.at[g * 12 + slot],
            g_recv.at[g * 12 + slot],
            toward(g, k, delta),
        )
        copy.start()
        sends.append(copy)

    def gather_wait(g, slot, start, count):
        remote(
            rows_at(start, count),
            rows_at(start, count),
            g_send.at[g * 12 + slot],
            g_recv.at[g * 12 + slot],
            sibling,
        ).wait_recv()

    def pass_on(g, slot, start, count):
        copy = remote(
            rows_at(start, count), rows_at(start, count), f_send.at[g * 7 + slot], f_recv.at[g * 7 + slot], sibling
        )
        copy.start()
        sends.append(copy)

    spots = []
    for g in range(GROUPS):
        spots.append(tuple(place(g, k) for k in range(3)))

    def finish_sum(g):
        for i in range(3):
            x_copies[g * 3 + i].wait_recv()
        summed = (
            chip_sum[g, pl.ds(pl.multiple_of(at["x"] * PIECE, PIECE), PIECE), :]
            + from_x[g, 0]
            + from_x[g, 1]
            + from_x[g, 2]
        )
        latent = summed[:, :RANK]
        power = jnp.mean(latent * latent, axis=1, keepdims=True)
        normed = latent * lax.rsqrt(power + eps_norm) * gain[...]
        tail = summed[:, RANK:]
        pair = jnp.concatenate([tail, tail], axis=1)
        swapped = jnp.where(lane < 32, pltpu.roll(pair, 96, 1), pltpu.roll(pair, 32, 1))
        cosine, sine = tables[g]
        turned = pair * cosine + swapped * sine
        own = base(g, core) + spots[g][2] * 256 + spots[g][1] * 64 + spots[g][0] * 16
        here = pl.ds(pl.multiple_of(own, PIECE), PIECE)
        buf[here, :RANK] = normed.astype(BF16)
        buf[here, RANK:] = turned.astype(BF16)

    def phase1(g):
        own = base(g, core) + spots[g][2] * 256 + spots[g][1] * 64 + spots[g][0] * 16
        for i, delta in enumerate(DELTAS):
            gather_send(g, i, own, PIECE, 0, delta)

    def line_at(x, c):
        return win.at[0, pl.ds(pl.multiple_of(4 * BLOCK + (x * 2 + c) * PIECE, PIECE), PIECE)]

    line_to = [moved("x", delta) for delta in DELTAS] + across + [sibling]

    def send_line():
        own = base(0, core) + spots[0][2] * 256 + spots[0][1] * 64 + spots[0][0] * 16
        for i, to in enumerate(line_to):
            copy = remote(rows_at(own, PIECE), line_at(at["x"], core), l_send.at[i], l_recv.at[i], to)
            copy.start()
            sends.append(copy)
        win[0, pl.ds(pl.multiple_of(4 * BLOCK + grp * PIECE, PIECE), PIECE), :] = buf[
            pl.ds(pl.multiple_of(own, PIECE), PIECE), :
        ]

    def wait_line():
        own = base(0, core) + spots[0][2] * 256 + spots[0][1] * 64 + spots[0][0] * 16
        for i in range(len(line_to)):
            x = at["x"] if i == 6 else lax.rem(at["x"] + 4 - DELTAS[i % 3], 4)
            c = core if i < 3 else other
            remote(rows_at(own, PIECE), line_at(x, c), l_send.at[i], l_recv.at[i], sibling).wait_recv()
        for k in range(8):
            target = 4 * BLOCK + k * PIECE
            piece = win[0, target : target + PIECE, :]
            win[1, target : target + PIECE, :] = pltpu.roll(piece.astype(F32), 64, 1).astype(BF16)

    def phase2(g):
        line = base(g, core) + spots[g][2] * 256 + spots[g][1] * 64
        for i, delta in enumerate(DELTAS):
            gather_wait(g, i, line + lax.rem(spots[g][0] + 4 - delta, 4) * 16, PIECE)
        for i, delta in enumerate(DELTAS):
            gather_send(g, 3 + i, line, 64, 1, delta)

    def half(g, offset, h):
        return base(g, core) + lax.rem(spots[g][2] + offset, 4) * 256 + h * 128

    def phase3(g):
        plane = base(g, core) + spots[g][2] * 256
        for i, delta in enumerate(DELTAS):
            gather_wait(g, 3 + i, plane + lax.rem(spots[g][1] + 4 - delta, 4) * 64, 64)
        gather_send(g, 6, half(g, 0, 0), 128, 2, 1)
        gather_send(g, 7, half(g, 0, 1), 128, 2, 3)
        gather_send(g, 8, half(g, 0, 1), 128, 2, 1)
        gather_send(g, 9, half(g, 0, 0), 128, 2, 3)
        pass_on(g, 0, plane, 256)

    def forward(g):
        gather_wait(g, 6, half(g, 3, 0), 128)
        gather_send(g, 10, half(g, 3, 0), 128, 2, 1)
        gather_wait(g, 7, half(g, 1, 1), 128)
        gather_send(g, 11, half(g, 1, 1), 128, 2, 3)
        pass_on(g, 1, half(g, 3, 0), 128)
        pass_on(g, 2, half(g, 1, 1), 128)

    def near(g):
        gather_wait(g, 8, half(g, 3, 1), 128)
        pass_on(g, 3, half(g, 3, 1), 128)
        gather_wait(g, 9, half(g, 1, 0), 128)
        pass_on(g, 4, half(g, 1, 0), 128)

    def far(g):
        gather_wait(g, 10, half(g, 2, 0), 128)
        pass_on(g, 5, half(g, 2, 0), 128)
        gather_wait(g, 11, half(g, 2, 1), 128)
        pass_on(g, 6, half(g, 2, 1), 128)

    def passed(g, slots):
        for slot in slots:
            count = 256 if slot == 0 else 128
            start = base(g, other)
            remote(
                rows_at(start, count), rows_at(start, count), f_send.at[g * 7 + slot], f_recv.at[g * 7 + slot], sibling
            ).wait_recv()

    def copy_window(g, slot, where):
        for x in range(4):
            for c in range(2):
                start = base(g, c)
                for axis, stride in zip(ORDERS[g][c], SLOT_STRIDE, strict=True):
                    start = start + (x if axis == "x" else where[axis]) * stride
                piece = buf[pl.ds(pl.multiple_of(start, PIECE), PIECE), :]
                target = slot * BLOCK + (x * 2 + c) * PIECE
                win[0, target : target + PIECE, :] = piece
                win[1, target : target + PIECE, :] = pltpu.roll(piece.astype(F32), 64, 1).astype(BF16)

    def prefill(b):
        first = ctx * 4 + b
        qrow = lax.broadcasted_iota(jnp.int32, (BLOCK, 2 * BLOCK), 0)
        kcol = lax.broadcasted_iota(jnp.int32, (BLOCK, 2 * BLOCK), 1)
        floor = jnp.where(first > 0, 0, BLOCK)
        allowed = (kcol >= floor) & (kcol - BLOCK <= qrow)
        mine = slice(b * BLOCK, (b + 1) * BLOCK)
        for odd in range(2):
            queries = jnp.concatenate(
                [q_v[mine, p * 2 * WIDTH + odd * RANK : p * 2 * WIDTH + odd * RANK + WIDE] for p in range(8)], axis=0
            )
            pre_s[odd] = dot_nt(queries, win[odd, b * BLOCK : (b + 2) * BLOCK, :])
        for odd in range(2):
            for p in range(8):
                rows = slice(p * BLOCK, (p + 1) * BLOCK)
                scores = jnp.where(allowed, pre_s[odd, rows], neg_fill)
                peak = jnp.max(scores, axis=1, keepdims=True)
                expo = jnp.exp2((scores - peak) * EXP2_SCALE)
                share = 1.0 / jnp.sum(expo, axis=1, keepdims=True)
                pre_w[odd, rows] = (expo * share).astype(BF16)
        values = win[0, b * BLOCK : (b + 2) * BLOCK, :RANK]
        for odd in range(2):
            latent = dot_nn(pre_w[odd], values).astype(BF16)
            for p in range(8):
                column = slice((2 * p + odd) * 128, (2 * p + odd + 1) * 128)
                result = dot_nn(latent[p * BLOCK : (p + 1) * BLOCK], uv_v[:, column])
                o_pre[mine, column] = result.astype(BF16)

    def decode_start():
        loads["qd"].wait()
        loads["kv"].wait()
        wide = lax.broadcasted_iota(jnp.int32, (PIECE, WIDE), 1)
        for h in range(DEC_HEADS):
            for s in range(2):
                column = (h // 2) * (2 * WIDTH) + (h % 2) * RANK
                piece = qd_v[s, :, column : column + WIDE].astype(F32)
                if h % 2:
                    piece = pltpu.roll(piece, WIDE - 64, 1)
                piece = jnp.where(wide < WIDTH, piece, 0.0)
                qs[h * 32 + s * 16 : h * 32 + (s + 1) * 16, :] = piece.astype(BF16)
        kn[...] = jnp.zeros_like(kn)
        for t in range(2):
            kn[t * 16 : (t + 1) * 16, :WIDTH] = kv_v[t]
        rows = lax.broadcasted_iota(jnp.int32, (256, 32), 0)
        cols = lax.broadcasted_iota(jnp.int32, (256, 32), 1)
        allowed = (lax.rem(rows, 16) == lax.rem(cols, 16)) & (cols // 16 <= lax.rem(rows, 32) // 16)
        scores = jnp.where(allowed, dot_nt(qs[...], kn[...]), neg_fill)
        peak = jnp.max(scores, axis=1, keepdims=True)
        expo = jnp.exp2((scores - peak) * EXP2_SCALE)
        top[...] = jnp.broadcast_to(peak, (256, 128))
        total[...] = jnp.broadcast_to(jnp.sum(expo, axis=1, keepdims=True), (256, 128))
        acc[...] = dot_nn(expo.astype(BF16), kn[:, :RANK])

    def decode(parts):
        attend(parts, at, lengths, buf, qs, acc, top, total)

    finish_sum(0)
    phase1(0)
    send_line()
    finish_sum(1)
    phase1(1)
    finish_sum(2)
    phase1(2)
    phase2(0)
    finish_sum(3)
    phase1(3)
    phase2(1)
    phase2(2)
    phase3(0)
    phase2(3)
    phase3(1)
    phase3(2)
    phase3(3)
    decode_start()
    forward(0)
    loads["q"].wait()
    loads["uv"].wait()
    wait_line()
    for g in range(GROUPS - 1):
        passed(g, (0,))
    passed(3, (0,))
    for g in range(1, GROUPS):
        copy_window(g, g, at)
    prefill(1)
    forward(1)
    forward(2)
    near(0)
    prefill(2)
    far(0)
    forward(3)
    prefill(3)
    near(1)
    near(2)
    passed(0, range(1, 7))
    behind = lax.rem(ctx + 15, 16)
    copy_window(0, 0, {"z": behind // 4, "y": lax.rem(behind, 4)})
    decode([(0, 0, None)])
    decode([(1, 0, None)])
    near(3)
    prefill(0)
    passed(1, range(1, 5))
    decode([(c, 1, offset) for c in range(2) for offset in (0, 1, 3)])
    far(1)
    far(2)
    passed(2, range(1, 5))
    decode([(c, 2, offset) for c in range(2) for offset in (0, 1, 3)])
    far(3)
    passed(3, range(1, 5))
    decode([(c, 3, offset) for c in range(2) for offset in (0, 1, 3)])
    for g in range(1, GROUPS):
        passed(g, range(5, 7))
    for copy in core_copies + x_copies + sends:
        copy.wait_send()


def finish(
    pre, buf, qs, acc_in, top_in, total_in, lengths, block_map, o_pre, o_cache, o_dec, acc, top, total, cache, flipped, dec, sems
):
    ctx = lax.axis_index("ctx")
    at = {"z": ctx // 4, "y": lax.rem(ctx, 4), "x": lax.axis_index("grp") // 2}
    pre_copy = pltpu.make_async_copy(pre, o_pre, sems.at[0])
    pre_copy.start()
    acc[...] = acc_in[...]
    top[...] = top_in[...]
    total[...] = total_in[...]
    attend([(c, g, 2) for c in range(2) for g in (1, 2, 3)], at, lengths, buf, qs, acc, top, total)
    result = (acc[...] / total[:, :1]).astype(BF16)
    for h in range(DEC_HEADS):
        for s in range(2):
            at_row = h * 32 + s * 16
            dec[s, :, h * RANK : (h + 1) * RANK] = result[at_row : at_row + 16]
    dec_copy = pltpu.make_async_copy(dec, o_dec, sems.at[1])
    dec_copy.start()

    def take_page(owner, carry):
        def look(j, found):
            return jnp.where(block_map[owner * 16 + j] == ctx, j, found)

        page = lax.fori_loop(0, 16, look, jnp.int32(0), unroll=True)
        row_block = page // 4
        where = {"x": lax.rem(page, 4), "y": lax.rem(owner, 4), "z": owner // 4}
        for c in range(2):
            start = jnp.int32(0)
            for k in range(GROUPS):
                here = base(k, c)
                for axis, stride in zip(ORDERS[k][c], SLOT_STRIDE, strict=True):
                    here = here + where[axis] * stride
                start = jnp.where(row_block == ROW_BLOCK[k], here, start)
            target = pl.multiple_of(owner * 32 + c * PIECE, PIECE)
            cache[pl.ds(target, PIECE), :] = buf[pl.ds(pl.multiple_of(start, PIECE), PIECE), :]
        return carry

    lax.fori_loop(0, 16, take_page, 0)
    flipped[...] = cache[...].T[:WIDTH]
    cache_copy = pltpu.make_async_copy(flipped, o_cache, sems.at[2])
    cache_copy.start()
    for copy in (pre_copy, dec_copy, cache_copy):
        copy.wait()


def shards(tokens, w_dkv, latent_gain, q_pre, w_uv, q_dec, kv_new, lengths, block_map):
    anywhere = pl.BlockSpec(memory_space=pl.ANY)
    vmem = pl.BlockSpec(memory_space=pltpu.VMEM)
    smem = pl.BlockSpec(memory_space=pltpu.SMEM)
    sems = pltpu.SemaphoreType.DMA
    results = pl.pallas_call(
        kernel,
        out_shape=(
            pltpu.VMEM((512, 2048), BF16),
            pltpu.VMEM((2 * GROUPS * GROUP_ROWS, WIDE), BF16),
            pltpu.VMEM((256, WIDE), BF16),
            pltpu.VMEM((256, RANK), F32),
            pltpu.VMEM((256, 128), F32),
            pltpu.VMEM((256, 128), F32),
        ),
        in_specs=[anywhere, anywhere, vmem, anywhere, anywhere, anywhere, anywhere, smem],
        out_specs=(vmem,) * 6,
        scratch_shapes=[
            pltpu.VMEM((512, 896), BF16),
            pltpu.VMEM((WIDTH, 896), BF16),
            pltpu.VMEM((512, HEADS * WIDTH), BF16),
            pltpu.VMEM((RANK, 2048), BF16),
            pltpu.VMEM((2, 16, DEC_HEADS * WIDTH), BF16),
            pltpu.VMEM((2, 16, WIDTH), BF16),
            pltpu.VMEM((GROUPS, 2, 64, WIDTH), F32),
            pltpu.VMEM((GROUPS, 64, WIDTH), F32),
            pltpu.VMEM((GROUPS, 64, WIDTH), F32),
            pltpu.VMEM((GROUPS, 3, PIECE, WIDTH), F32),
            pltpu.VMEM((2, 5 * BLOCK, WIDE), BF16),
            pltpu.VMEM((32, WIDE), BF16),
            pltpu.VMEM((2, 1024, 256), F32),
            pltpu.VMEM((2, 1024, 256), BF16),
            sems((6,)),
            sems((GROUPS,)),
            sems((GROUPS,)),
            sems((GROUPS * 3,)),
            sems((GROUPS * 3,)),
            sems((GROUPS * 12,)),
            sems((GROUPS * 12,)),
            sems((GROUPS * 7,)),
            sems((GROUPS * 7,)),
            sems((7,)),
            sems((7,)),
        ],
        compiler_params=pltpu.CompilerParams(
            collective_id=0, has_side_effects=True, vmem_limit_bytes=48 * 1024 * 1024
        ),
    )(tokens, w_dkv.T, latent_gain.reshape(1, RANK), q_pre, w_uv, q_dec, kv_new, lengths)
    pre, cache, dec = pl.pallas_call(
        finish,
        out_shape=(
            jax.ShapeDtypeStruct((512, 2048), BF16),
            jax.ShapeDtypeStruct((WIDTH, 512), BF16),
            jax.ShapeDtypeStruct((2, 16, 4096), BF16),
        ),
        in_specs=[vmem] * 6 + [smem, smem],
        out_specs=(anywhere, anywhere, anywhere),
        scratch_shapes=[
            pltpu.VMEM((256, RANK), F32),
            pltpu.VMEM((256, 128), F32),
            pltpu.VMEM((256, 128), F32),
            pltpu.VMEM((512, WIDE), BF16),
            pltpu.VMEM((WIDTH, 512), BF16),
            pltpu.VMEM((2, 16, 4096), BF16),
            sems((3,)),
        ],
        compiler_params=pltpu.CompilerParams(vmem_limit_bytes=24 * 1024 * 1024),
    )(*results, lengths, block_map)
    return pre, cache.T, dec


def solution(mesh):
    placed = (
        P("ctx", "grp"),
        P("grp", None),
        P(),
        P("ctx", "grp"),
        P(None, "grp"),
        P(None, "grp", None),
        P(None, "grp", None),
        P("grp"),
        P(),
    )
    return jax.shard_map(
        shards,
        mesh=mesh,
        in_specs=placed,
        out_specs=(P("ctx", "grp"), P("ctx", None), P(None, "grp", "ctx")),
        check_vma=False,
    )
```

```python
import math

import jax
import jax.numpy as jnp
import numpy as np
from jax import lax
from jax.experimental import pallas as pl
from jax.experimental.pallas import tpu as pltpu
from jax.sharding import PartitionSpec as P

MESH = pl.DeviceIdType.MESH
F32 = jnp.float32
BF16 = jnp.bfloat16

scale_qk = 0.07216878364870322
eps_norm = 1e-06
neg_fill = -1e30
EXP2_SCALE = scale_qk * math.log2(math.e)

RANK = 512
WIDTH = 576
WIDE = 640
ROPE = 64
BLOCK = 128
PIECE = 16
GROUPS = 4
GROUP_ROWS = 1024
HEADS = 16
DEC_HEADS = 8

ORDERS = (
    ("yzx", "zyx"),
    ("zxy", "xzy"),
    ("yxz", "xyz"),
    ("xzy", "xyz"),
)
ROW_BLOCK = (3, 0, 1, 2)
POS_STRIDE = {"z": 2048, "y": 512, "x": 32}
SLOT_STRIDE = (PIECE, 4 * PIECE, 16 * PIECE)
DELTAS = (1, 3, 2)
FREQS = [float(np.float32(10000.0 ** (-2.0 * i / ROPE))) for i in range(ROPE // 2)]


def dot_nt(a, b):
    return lax.dot_general(a, b, (((1,), (1,)), ((), ())), preferred_element_type=F32)


def dot_nn(a, b):
    return jnp.dot(a, b, preferred_element_type=F32)


def base(g, plane):
    return (plane * GROUPS + g) * GROUP_ROWS


def attend(parts, at, lengths, buf, qs, acc, top, total):
    request = lax.rem(lax.broadcasted_iota(jnp.int32, (256, 1), 0), 16)
    limit = jnp.zeros((256, 1), jnp.int32)
    for r in range(16):
        limit = jnp.where(request == r, lengths[r], limit)
    spans, masks = [], []
    for plane, g, offset in parts:
        order = ORDERS[g][plane]
        count = GROUP_ROWS if offset is None else 256
        last = 0 if offset is None else lax.rem(at[order[2]] + offset, 4)
        spans.append(pl.ds(pl.multiple_of(base(g, plane) + last * 256, 256), count))
        key = lax.broadcasted_iota(jnp.int32, (1, count), 1)
        position = ROW_BLOCK[g] * BLOCK + plane * PIECE + lax.rem(key, PIECE) + last * POS_STRIDE[order[2]]
        for axis, stride in zip(order, SLOT_STRIDE, strict=True):
            position = position + lax.rem(key // stride, 4) * POS_STRIDE[axis]
        masks.append(position < limit)
    keys = jnp.concatenate([buf[span, :] for span in spans], axis=0)
    scores = dot_nt(qs[...], keys)
    scores = jnp.where(jnp.concatenate(masks, axis=1), scores, neg_fill)
    before = top[:, :1]
    peak = jnp.maximum(before, jnp.max(scores, axis=1, keepdims=True))
    factor = jnp.exp2((before - peak) * EXP2_SCALE)
    expo = jnp.exp2((scores - peak) * EXP2_SCALE)
    top[...] = jnp.broadcast_to(peak, (256, 128))
    total[...] = total[...] * factor + jnp.sum(expo, axis=1, keepdims=True)
    values = jnp.concatenate([buf[span, :RANK] for span in spans], axis=0)
    acc[...] = acc[...] * factor + dot_nn(expo.astype(BF16), values)


def kernel(
    tokens,
    w_dkv,
    gain,
    q_pre,
    w_uv,
    q_dec,
    kv_new,
    lengths,
    o_pre,
    buf,
    qs,
    acc,
    top,
    total,
    tok_v,
    w_v,
    q_v,
    uv_v,
    qd_v,
    kv_v,
    part,
    from_core,
    chip_sum,
    from_x,
    win,
    kn,
    pre_s,
    pre_w,
    load_sem,
    core_send,
    core_recv,
    x_send,
    x_recv,
    g_send,
    g_recv,
    f_send,
    f_recv,
    l_send,
    l_recv,
):
    ctx = lax.axis_index("ctx")
    grp = lax.axis_index("grp")
    at = {"z": ctx // 4, "y": lax.rem(ctx, 4), "x": grp // 2}
    core = lax.rem(grp, 2)
    other = 1 - core

    def device(x, y, z, c):
        return (z * 4 + y, x * 2 + c)

    def moved(axis, delta):
        new = dict(at)
        new[axis] = lax.rem(at[axis] + delta, 4)
        return device(new["x"], new["y"], new["z"], core)

    sibling = device(at["x"], at["y"], at["z"], other)

    loads = {
        "tok": pltpu.make_async_copy(tokens, tok_v, load_sem.at[0]),
        "w": pltpu.make_async_copy(w_dkv, w_v, load_sem.at[1]),
        "qd": pltpu.make_async_copy(
            q_dec.at[:, :, pl.ds(pl.multiple_of(ctx * (DEC_HEADS * WIDTH), 128), DEC_HEADS * WIDTH)],
            qd_v,
            load_sem.at[2],
        ),
        "kv": pltpu.make_async_copy(kv_new, kv_v, load_sem.at[3]),
        "q": pltpu.make_async_copy(q_pre, q_v, load_sem.at[4]),
        "uv": pltpu.make_async_copy(w_uv, uv_v, load_sem.at[5]),
    }
    loads["tok"].start()
    loads["w"].start()

    barrier = pltpu.get_barrier_semaphore()
    across = [device(lax.rem(at["x"] + delta, 4), at["y"], at["z"], other) for delta in DELTAS]
    peers = [sibling] + across + [moved(axis, delta) for axis in "xyz" for delta in DELTAS]
    for peer in peers:
        pl.semaphore_signal(barrier, inc=1, device_id=peer, device_id_type=MESH)

    def remote(src, dst, send, recv, to):
        return pltpu.make_async_remote_copy(
            src_ref=src, dst_ref=dst, send_sem=send, recv_sem=recv, device_id=to, device_id_type=MESH
        )

    lane = lax.broadcasted_iota(jnp.int32, (PIECE, 128), 1)
    row = lax.broadcasted_iota(jnp.int32, (PIECE, 128), 0)
    freq = jnp.zeros((PIECE, 128), F32)
    for i, value in enumerate(FREQS):
        freq = jnp.where(lane % 32 == i, value, freq)
    tables = []
    for g in range(GROUPS):
        position = ctx * 512 + ROW_BLOCK[g] * BLOCK + grp * PIECE + row
        angle = position.astype(F32) * freq
        cosine = jnp.where(lane < ROPE, jnp.cos(angle), 0.0)
        sine = jnp.where(lane < ROPE, jnp.sin(angle), 0.0)
        tables.append((cosine, jnp.where(lane < 32, -sine, sine)))

    loads["tok"].wait()
    loads["w"].wait()
    for name in ("qd", "kv", "q", "uv"):
        loads[name].start()

    core_copies = []
    x_copies = []

    def project(g):
        first = ROW_BLOCK[g] * BLOCK
        product = dot_nt(tok_v[first : first + BLOCK, :], w_v[...])
        for x in range(4):
            for c in range(2):
                at_row = (x * 2 + c) * PIECE
                part[g, c, x * PIECE : (x + 1) * PIECE, :] = product[at_row : at_row + PIECE]

    def to_core(g):
        copy = remote(part.at[g, other], from_core.at[g], core_send.at[g], core_recv.at[g], sibling)
        copy.start()
        core_copies.append(copy)

    def to_x(g):
        core_copies[g].wait_recv()
        chip_sum[g] = part[g, core] + from_core[g]
        for i, delta in enumerate(DELTAS):
            target = lax.rem(at["x"] + delta, 4)
            copy = remote(
                chip_sum.at[g, pl.ds(pl.multiple_of(target * PIECE, PIECE), PIECE)],
                from_x.at[g, i],
                x_send.at[g * 3 + i],
                x_recv.at[g * 3 + i],
                moved("x", delta),
            )
            copy.start()
            x_copies.append(copy)

    project(0)
    pl.semaphore_wait(barrier, len(peers))
    to_core(0)
    project(1)
    to_core(1)
    project(2)
    to_core(2)
    to_x(0)
    project(3)
    to_core(3)
    for g in range(1, GROUPS):
        to_x(g)

    sends = []

    def place(g, k):
        first, second = ORDERS[g][0][k], ORDERS[g][1][k]
        if first == second:
            return at[first]
        return jnp.where(core == 0, at[first], at[second])

    def toward(g, k, delta):
        first, second = ORDERS[g][0][k], ORDERS[g][1][k]
        new = dict(at)
        if first == second:
            new[first] = lax.rem(at[first] + delta, 4)
        else:
            new[first] = lax.rem(at[first] + delta * (1 - core), 4)
            new[second] = lax.rem(at[second] + delta * core, 4)
        return device(new["x"], new["y"], new["z"], core)

    def rows_at(start, count):
        return buf.at[pl.ds(pl.multiple_of(start, PIECE), count)]

    def gather_send(g, slot, start, count, k, delta):
        copy = remote(
            rows_at(start, count),
            rows_at(start, count),
            g_send.at[g * 12 + slot],
            g_recv.at[g * 12 + slot],
            toward(g, k, delta),
        )
        copy.start()
        sends.append(copy)

    def gather_wait(g, slot, start, count):
        remote(
            rows_at(start, count),
            rows_at(start, count),
            g_send.at[g * 12 + slot],
            g_recv.at[g * 12 + slot],
            sibling,
        ).wait_recv()

    def pass_on(g, slot, start, count):
        copy = remote(
            rows_at(start, count), rows_at(start, count), f_send.at[g * 7 + slot], f_recv.at[g * 7 + slot], sibling
        )
        copy.start()
        sends.append(copy)

    spots = []
    for g in range(GROUPS):
        spots.append(tuple(place(g, k) for k in range(3)))

    def finish_sum(g):
        for i in range(3):
            x_copies[g * 3 + i].wait_recv()
        summed = (
            chip_sum[g, pl.ds(pl.multiple_of(at["x"] * PIECE, PIECE), PIECE), :]
            + from_x[g, 0]
            + from_x[g, 1]
            + from_x[g, 2]
        )
        latent = summed[:, :RANK]
        power = jnp.mean(latent * latent, axis=1, keepdims=True)
        normed = latent * lax.rsqrt(power + eps_norm) * gain[...]
        tail = summed[:, RANK:]
        pair = jnp.concatenate([tail, tail], axis=1)
        swapped = jnp.where(lane < 32, pltpu.roll(pair, 96, 1), pltpu.roll(pair, 32, 1))
        cosine, sine = tables[g]
        turned = pair * cosine + swapped * sine
        own = base(g, core) + spots[g][2] * 256 + spots[g][1] * 64 + spots[g][0] * 16
        here = pl.ds(pl.multiple_of(own, PIECE), PIECE)
        buf[here, :RANK] = normed.astype(BF16)
        buf[here, RANK:] = turned.astype(BF16)

    def phase1(g):
        own = base(g, core) + spots[g][2] * 256 + spots[g][1] * 64 + spots[g][0] * 16
        for i, delta in enumerate(DELTAS):
            gather_send(g, i, own, PIECE, 0, delta)

    def line_at(x, c):
        return win.at[0, pl.ds(pl.multiple_of(4 * BLOCK + (x * 2 + c) * PIECE, PIECE), PIECE)]

    line_to = [moved("x", delta) for delta in DELTAS] + across + [sibling]

    def send_line():
        own = base(0, core) + spots[0][2] * 256 + spots[0][1] * 64 + spots[0][0] * 16
        for i, to in enumerate(line_to):
            copy = remote(rows_at(own, PIECE), line_at(at["x"], core), l_send.at[i], l_recv.at[i], to)
            copy.start()
            sends.append(copy)
        win[0, pl.ds(pl.multiple_of(4 * BLOCK + grp * PIECE, PIECE), PIECE), :] = buf[
            pl.ds(pl.multiple_of(own, PIECE), PIECE), :
        ]

    def wait_line():
        own = base(0, core) + spots[0][2] * 256 + spots[0][1] * 64 + spots[0][0] * 16
        for i in range(len(line_to)):
            x = at["x"] if i == 6 else lax.rem(at["x"] + 4 - DELTAS[i % 3], 4)
            c = core if i < 3 else other
            remote(rows_at(own, PIECE), line_at(x, c), l_send.at[i], l_recv.at[i], sibling).wait_recv()
        for k in range(8):
            target = 4 * BLOCK + k * PIECE
            piece = win[0, target : target + PIECE, :]
            win[1, target : target + PIECE, :] = pltpu.roll(piece.astype(F32), 64, 1).astype(BF16)

    def phase2(g):
        line = base(g, core) + spots[g][2] * 256 + spots[g][1] * 64
        for i, delta in enumerate(DELTAS):
            gather_wait(g, i, line + lax.rem(spots[g][0] + 4 - delta, 4) * 16, PIECE)
        for i, delta in enumerate(DELTAS):
            gather_send(g, 3 + i, line, 64, 1, delta)

    def half(g, offset, h):
        return base(g, core) + lax.rem(spots[g][2] + offset, 4) * 256 + h * 128

    def phase3(g):
        plane = base(g, core) + spots[g][2] * 256
        for i, delta in enumerate(DELTAS):
            gather_wait(g, 3 + i, plane + lax.rem(spots[g][1] + 4 - delta, 4) * 64, 64)
        gather_send(g, 6, half(g, 0, 0), 128, 2, 1)
        gather_send(g, 7, half(g, 0, 1), 128, 2, 3)
        gather_send(g, 8, half(g, 0, 1), 128, 2, 1)
        gather_send(g, 9, half(g, 0, 0), 128, 2, 3)
        pass_on(g, 0, plane, 256)

    def forward(g):
        gather_wait(g, 6, half(g, 3, 0), 128)
        gather_send(g, 10, half(g, 3, 0), 128, 2, 1)
        gather_wait(g, 7, half(g, 1, 1), 128)
        gather_send(g, 11, half(g, 1, 1), 128, 2, 3)
        pass_on(g, 1, half(g, 3, 0), 128)
        pass_on(g, 2, half(g, 1, 1), 128)

    def near(g):
        gather_wait(g, 8, half(g, 3, 1), 128)
        pass_on(g, 3, half(g, 3, 1), 128)
        gather_wait(g, 9, half(g, 1, 0), 128)
        pass_on(g, 4, half(g, 1, 0), 128)

    def far(g):
        gather_wait(g, 10, half(g, 2, 0), 128)
        pass_on(g, 5, half(g, 2, 0), 128)
        gather_wait(g, 11, half(g, 2, 1), 128)
        pass_on(g, 6, half(g, 2, 1), 128)

    def passed(g, slots):
        for slot in slots:
            count = 256 if slot == 0 else 128
            start = base(g, other)
            remote(
                rows_at(start, count), rows_at(start, count), f_send.at[g * 7 + slot], f_recv.at[g * 7 + slot], sibling
            ).wait_recv()

    def copy_window(g, slot, where):
        for x in range(4):
            for c in range(2):
                start = base(g, c)
                for axis, stride in zip(ORDERS[g][c], SLOT_STRIDE, strict=True):
                    start = start + (x if axis == "x" else where[axis]) * stride
                piece = buf[pl.ds(pl.multiple_of(start, PIECE), PIECE), :]
                target = slot * BLOCK + (x * 2 + c) * PIECE
                win[0, target : target + PIECE, :] = piece
                win[1, target : target + PIECE, :] = pltpu.roll(piece.astype(F32), 64, 1).astype(BF16)

    def prefill(b):
        first = ctx * 4 + b
        qrow = lax.broadcasted_iota(jnp.int32, (BLOCK, 2 * BLOCK), 0)
        kcol = lax.broadcasted_iota(jnp.int32, (BLOCK, 2 * BLOCK), 1)
        floor = jnp.where(first > 0, 0, BLOCK)
        allowed = (kcol >= floor) & (kcol - BLOCK <= qrow)
        mine = slice(b * BLOCK, (b + 1) * BLOCK)
        for odd in range(2):
            queries = jnp.concatenate(
                [q_v[mine, p * 2 * WIDTH + odd * RANK : p * 2 * WIDTH + odd * RANK + WIDE] for p in range(8)], axis=0
            )
            pre_s[odd] = dot_nt(queries, win[odd, b * BLOCK : (b + 2) * BLOCK, :])
        for odd in range(2):
            for p in range(8):
                rows = slice(p * BLOCK, (p + 1) * BLOCK)
                scores = jnp.where(allowed, pre_s[odd, rows], neg_fill)
                peak = jnp.max(scores, axis=1, keepdims=True)
                expo = jnp.exp2((scores - peak) * EXP2_SCALE)
                share = 1.0 / jnp.sum(expo, axis=1, keepdims=True)
                pre_w[odd, rows] = (expo * share).astype(BF16)
        values = win[0, b * BLOCK : (b + 2) * BLOCK, :RANK]
        for odd in range(2):
            latent = dot_nn(pre_w[odd], values).astype(BF16)
            for p in range(8):
                column = slice((2 * p + odd) * 128, (2 * p + odd + 1) * 128)
                result = dot_nn(latent[p * BLOCK : (p + 1) * BLOCK], uv_v[:, column])
                o_pre[mine, column] = result.astype(BF16)

    def decode_start():
        loads["qd"].wait()
        loads["kv"].wait()
        wide = lax.broadcasted_iota(jnp.int32, (PIECE, WIDE), 1)
        for h in range(DEC_HEADS):
            for s in range(2):
                column = (h // 2) * (2 * WIDTH) + (h % 2) * RANK
                piece = qd_v[s, :, column : column + WIDE].astype(F32)
                if h % 2:
                    piece = pltpu.roll(piece, WIDE - 64, 1)
                piece = jnp.where(wide < WIDTH, piece, 0.0)
                qs[h * 32 + s * 16 : h * 32 + (s + 1) * 16, :] = piece.astype(BF16)
        kn[...] = jnp.zeros_like(kn)
        for t in range(2):
            kn[t * 16 : (t + 1) * 16, :WIDTH] = kv_v[t]
        rows = lax.broadcasted_iota(jnp.int32, (256, 32), 0)
        cols = lax.broadcasted_iota(jnp.int32, (256, 32), 1)
        allowed = (lax.rem(rows, 16) == lax.rem(cols, 16)) & (cols // 16 <= lax.rem(rows, 32) // 16)
        scores = jnp.where(allowed, dot_nt(qs[...], kn[...]), neg_fill)
        peak = jnp.max(scores, axis=1, keepdims=True)
        expo = jnp.exp2((scores - peak) * EXP2_SCALE)
        top[...] = jnp.broadcast_to(peak, (256, 128))
        total[...] = jnp.broadcast_to(jnp.sum(expo, axis=1, keepdims=True), (256, 128))
        acc[...] = dot_nn(expo.astype(BF16), kn[:, :RANK])

    def decode(parts):
        attend(parts, at, lengths, buf, qs, acc, top, total)

    finish_sum(0)
    phase1(0)
    send_line()
    finish_sum(1)
    phase1(1)
    finish_sum(2)
    phase1(2)
    phase2(0)
    finish_sum(3)
    phase1(3)
    phase2(1)
    phase2(2)
    phase3(0)
    phase2(3)
    phase3(1)
    phase3(2)
    phase3(3)
    decode_start()
    forward(0)
    loads["q"].wait()
    loads["uv"].wait()
    wait_line()
    for g in range(GROUPS - 1):
        passed(g, (0,))
    passed(3, (0,))
    for g in range(1, GROUPS):
        copy_window(g, g, at)
    prefill(1)
    forward(1)
    forward(2)
    near(0)
    prefill(2)
    far(0)
    forward(3)
    prefill(3)
    near(1)
    near(2)
    passed(0, range(1, 7))
    behind = lax.rem(ctx + 15, 16)
    copy_window(0, 0, {"z": behind // 4, "y": lax.rem(behind, 4)})
    decode([(0, 0, None)])
    decode([(1, 0, None)])
    prefill(0)
    passed(1, range(1, 5))
    decode([(c, 1, offset) for c in range(2) for offset in (0, 1, 3)])
    near(3)
    far(1)
    passed(2, range(1, 5))
    decode([(c, 2, offset) for c in range(2) for offset in (0, 1, 3)])
    far(2)
    passed(3, range(1, 5))
    decode([(c, 3, offset) for c in range(2) for offset in (0, 1, 3)])
    far(3)
    for g in range(1, GROUPS):
        passed(g, range(5, 7))
    for copy in core_copies + x_copies + sends:
        copy.wait_send()


def finish(
    pre, buf, qs, acc_in, top_in, total_in, lengths, block_map, o_pre, o_cache, o_dec, acc, top, total, cache, flipped, dec, sems
):
    ctx = lax.axis_index("ctx")
    at = {"z": ctx // 4, "y": lax.rem(ctx, 4), "x": lax.axis_index("grp") // 2}
    pre_copy = pltpu.make_async_copy(pre, o_pre, sems.at[0])
    pre_copy.start()
    acc[...] = acc_in[...]
    top[...] = top_in[...]
    total[...] = total_in[...]
    attend([(c, g, 2) for c in range(2) for g in (1, 2, 3)], at, lengths, buf, qs, acc, top, total)
    result = (acc[...] / total[:, :1]).astype(BF16)
    for h in range(DEC_HEADS):
        for s in range(2):
            at_row = h * 32 + s * 16
            dec[s, :, h * RANK : (h + 1) * RANK] = result[at_row : at_row + 16]
    dec_copy = pltpu.make_async_copy(dec, o_dec, sems.at[1])
    dec_copy.start()

    def take_page(owner, carry):
        def look(j, found):
            return jnp.where(block_map[owner * 16 + j] == ctx, j, found)

        page = lax.fori_loop(0, 16, look, jnp.int32(0), unroll=True)
        row_block = page // 4
        where = {"x": lax.rem(page, 4), "y": lax.rem(owner, 4), "z": owner // 4}
        for c in range(2):
            start = jnp.int32(0)
            for k in range(GROUPS):
                here = base(k, c)
                for axis, stride in zip(ORDERS[k][c], SLOT_STRIDE, strict=True):
                    here = here + where[axis] * stride
                start = jnp.where(row_block == ROW_BLOCK[k], here, start)
            target = pl.multiple_of(owner * 32 + c * PIECE, PIECE)
            cache[pl.ds(target, PIECE), :] = buf[pl.ds(pl.multiple_of(start, PIECE), PIECE), :]
        return carry

    lax.fori_loop(0, 16, take_page, 0)
    flipped[...] = cache[...].T[:WIDTH]
    cache_copy = pltpu.make_async_copy(flipped, o_cache, sems.at[2])
    cache_copy.start()
    for copy in (pre_copy, dec_copy, cache_copy):
        copy.wait()


def shards(tokens, w_dkv, latent_gain, q_pre, w_uv, q_dec, kv_new, lengths, block_map):
    anywhere = pl.BlockSpec(memory_space=pl.ANY)
    vmem = pl.BlockSpec(memory_space=pltpu.VMEM)
    smem = pl.BlockSpec(memory_space=pltpu.SMEM)
    sems = pltpu.SemaphoreType.DMA
    results = pl.pallas_call(
        kernel,
        out_shape=(
            pltpu.VMEM((512, 2048), BF16),
            pltpu.VMEM((2 * GROUPS * GROUP_ROWS, WIDE), BF16),
            pltpu.VMEM((256, WIDE), BF16),
            pltpu.VMEM((256, RANK), F32),
            pltpu.VMEM((256, 128), F32),
            pltpu.VMEM((256, 128), F32),
        ),
        in_specs=[anywhere, anywhere, vmem, anywhere, anywhere, anywhere, anywhere, smem],
        out_specs=(vmem,) * 6,
        scratch_shapes=[
            pltpu.VMEM((512, 896), BF16),
            pltpu.VMEM((WIDTH, 896), BF16),
            pltpu.VMEM((512, HEADS * WIDTH), BF16),
            pltpu.VMEM((RANK, 2048), BF16),
            pltpu.VMEM((2, 16, DEC_HEADS * WIDTH), BF16),
            pltpu.VMEM((2, 16, WIDTH), BF16),
            pltpu.VMEM((GROUPS, 2, 64, WIDTH), F32),
            pltpu.VMEM((GROUPS, 64, WIDTH), F32),
            pltpu.VMEM((GROUPS, 64, WIDTH), F32),
            pltpu.VMEM((GROUPS, 3, PIECE, WIDTH), F32),
            pltpu.VMEM((2, 5 * BLOCK, WIDE), BF16),
            pltpu.VMEM((32, WIDE), BF16),
            pltpu.VMEM((2, 1024, 256), F32),
            pltpu.VMEM((2, 1024, 256), BF16),
            sems((6,)),
            sems((GROUPS,)),
            sems((GROUPS,)),
            sems((GROUPS * 3,)),
            sems((GROUPS * 3,)),
            sems((GROUPS * 12,)),
            sems((GROUPS * 12,)),
            sems((GROUPS * 7,)),
            sems((GROUPS * 7,)),
            sems((7,)),
            sems((7,)),
        ],
        compiler_params=pltpu.CompilerParams(
            collective_id=0, has_side_effects=True, vmem_limit_bytes=48 * 1024 * 1024
        ),
    )(tokens, w_dkv.T, latent_gain.reshape(1, RANK), q_pre, w_uv, q_dec, kv_new, lengths)
    pre, cache, dec = pl.pallas_call(
        finish,
        out_shape=(
            jax.ShapeDtypeStruct((512, 2048), BF16),
            jax.ShapeDtypeStruct((WIDTH, 512), BF16),
            jax.ShapeDtypeStruct((2, 16, 4096), BF16),
        ),
        in_specs=[vmem] * 6 + [smem, smem],
        out_specs=(anywhere, anywhere, anywhere),
        scratch_shapes=[
            pltpu.VMEM((256, RANK), F32),
            pltpu.VMEM((256, 128), F32),
            pltpu.VMEM((256, 128), F32),
            pltpu.VMEM((512, WIDE), BF16),
            pltpu.VMEM((WIDTH, 512), BF16),
            pltpu.VMEM((2, 16, 4096), BF16),
            sems((3,)),
        ],
        compiler_params=pltpu.CompilerParams(vmem_limit_bytes=24 * 1024 * 1024),
    )(*results, lengths, block_map)
    return pre, cache.T, dec


def solution(mesh):
    placed = (
        P("ctx", "grp"),
        P("grp", None),
        P(),
        P("ctx", "grp"),
        P(None, "grp"),
        P(None, "grp", None),
        P(None, "grp", None),
        P("grp"),
        P(),
    )
    return jax.shard_map(
        shards,
        mesh=mesh,
        in_specs=placed,
        out_specs=(P("ctx", "grp"), P("ctx", None), P(None, "grp", "ctx")),
        check_vma=False,
    )
```
